512 devices in a mesh: gx: 64 (over x, z, core), gy: 8 (over y).
Axes of the slice: x: 4, y: 8, z: 8, core: 2. Of those that a mesh axis runs over, the one named last changes fastest.
Arguments:
- source: float32 [1024, 256, 128], P('gx', 'gy'), may hold values from -6 to 6
- tissue: int32 [1024, 256, 128], P('gx', 'gy'), may hold values from 0 to 7
- diffusivity: float32 [8], replicated, may hold values from 0.2 to 5
- uptake: float32 [8], replicated, may hold values from 0.002 to 0.05
Outputs:
- ligand: float32 [1024, 256, 128], P('gx', 'gy')
The draws below stay inside these ranges and needn't reach their ends.
All inputs are finite; a program needn't handle non-finite values.
Results may differ from the reference program's by a relative error of at most 0.00002.
Values sent between devices are 32-bit elements; how exact they have to be, the bound alone decides.
A program may use at most 64 MiB of HBM per device.

```python
import math
import jax
import jax.numpy as jnp

LEVELS = 6
TYPES = 8
COARSE = 4
NX = 1024
NY = 256
NZ = 128


def touch_ends(array, stream_key, low, largest):
    longest = array.shape.index(max(array.shape))
    spots = []
    for shift in (0, 1):
        where = [jax.random.randint(jax.random.fold_in(stream_key, axis), (), 0, length) for axis, length in enumerate(array.shape)]
        where[longest] = (where[longest] + shift) % array.shape[longest]
        spots.append(tuple(where))
    return array.at[spots[0]].set(low).at[spots[1]].set(largest)


def block_levels(rng, dims, split, smallest, top_value):
    def one(position, blocks):
        draws = jax.random.uniform(jax.random.fold_in(jax.random.fold_in(rng, 6), position), (blocks,), jnp.float32, smallest / len(split), top_value / len(split))
        return jnp.repeat(jnp.exp(draws), dims[position] // blocks).reshape((-1,) + (1,) * (len(dims) - position - 1))

    level = one(*split[0])
    for cut in split[1:]:
        level = level * one(*cut)
    return level


def centred(own_key, shape, deviation, most, cuts=(), dtype=jnp.bfloat16):
    values = deviation * jax.random.normal(own_key, shape, jnp.float32)
    if cuts:
        values = values * block_levels(own_key, shape, cuts, -0.22, 0.18)
    return jnp.clip(values, -most, most).astype(dtype)


def setup_inputs(seed: int = 0) -> dict:
    streams_of = jax.random.split(jax.random.key(seed), 5)
    return {
        "source": centred(streams_of[0], (NX, NY, NZ), 1.0, 6.0, ((0, 64), (1, 8)), jnp.float32),
        "tissue": touch_ends(jax.random.randint(streams_of[1], (NX, NY, NZ), 0, TYPES), jax.random.fold_in(streams_of[1], 1), 0, TYPES - 1).astype(jnp.int32),
        "diffusivity": jnp.clip(jnp.exp(jax.random.uniform(streams_of[2], (TYPES,), jnp.float32, math.log(0.2), math.log(5.0))), 0.2, 5.0),
        "uptake": jnp.clip(jnp.exp(jax.random.uniform(streams_of[3], (TYPES,), jnp.float32, math.log(0.002), math.log(0.05))), 0.002, 0.05),
    }


OMEGA = 0.8
ZFACE = 0.015625


def operate(u_pad, kap_pad, sig, scale):
    kc = kap_pad[1:-1, 1:-1]
    core = u_pad[1:-1, 1:-1]
    east = (0.5 * scale) * (kc + kap_pad[2:, 1:-1])
    west = (0.5 * scale) * (kc + kap_pad[:-2, 1:-1])
    north = (0.5 * scale) * (kc + kap_pad[1:-1, 2:])
    south = (0.5 * scale) * (kc + kap_pad[1:-1, :-2])
    kap_z = jnp.pad(kc, ((0, 0), (0, 0), (1, 1)))
    upper = (0.5 * ZFACE) * (kc + kap_z[:, :, 2:])
    lower = (0.5 * ZFACE) * (kc + kap_z[:, :, :-2])
    core_z = jnp.pad(core, ((0, 0), (0, 0), (1, 1)))
    diag = east + west + north + south + upper + lower + sig
    pulled = (east * u_pad[2:, 1:-1] + west * u_pad[:-2, 1:-1] + north * u_pad[1:-1, 2:]
              + south * u_pad[1:-1, :-2] + upper * core_z[:, :, 2:] + lower * core_z[:, :, :-2])
    return diag, diag * core - pulled


def relax(u_pad, rhs, kap_pad, sig, scale):
    diag, applied = operate(u_pad, kap_pad, sig, scale)
    return u_pad[1:-1, 1:-1] + OMEGA * (rhs - applied) / diag


def restrict(field):
    return 0.25 * ((field[0::2, 0::2] + field[1::2, 0::2]) + (field[0::2, 1::2] + field[1::2, 1::2]))


def prolong(field):
    return jnp.repeat(jnp.repeat(field, 2, axis=0), 2, axis=1)


def border(field):
    return jnp.pad(field, ((1, 1), (1, 1), (0, 0)))


def reference(source, tissue, diffusivity, uptake):
    kappa = diffusivity[tissue]
    sigma = uptake[tissue]
    rhs = source
    saved = []
    for level in range(LEVELS - 1):
        scale = 0.25 ** level
        kap_pad = border(kappa)
        smooth = relax(border(jnp.zeros_like(rhs)), rhs, kap_pad, sigma, scale)
        smooth = relax(border(smooth), rhs, kap_pad, sigma, scale)
        diag, applied = operate(border(smooth), kap_pad, sigma, scale)
        saved.append((smooth, rhs, kap_pad, sigma, scale))
        rhs = restrict(rhs - applied)
        kappa = restrict(kappa)
        sigma = restrict(sigma)
    scale = 0.25 ** (LEVELS - 1)
    kap_pad = border(kappa)
    result = relax(border(jnp.zeros_like(rhs)), rhs, kap_pad, sigma, scale)
    for turn in range(COARSE - 1):
        result = relax(border(result), rhs, kap_pad, sigma, scale)
    for level in reversed(range(LEVELS - 1)):
        smooth, rhs, kap_pad, sigma, scale = saved[level]
        result = smooth + prolong(result)
        for turn in range(2):
            result = relax(border(result), rhs, kap_pad, sigma, scale)
    return result
```

```python
import functools

import jax
import jax.numpy as jnp
from jax import lax
from jax.experimental import pallas as pl
from jax.experimental.pallas import tpu as pltpu
from jax.sharding import PartitionSpec as P

MESH = pl.DeviceIdType.MESH
F32 = jnp.float32
LEVELS = 6
TYPES = 8
HZ = 0.5 * 0.015625
REACH = (3, 4, 5, 5, 5, 5)


class Level:
    def __init__(self, index, rows, columns, across, blk):
        self.index, self.rows, self.columns, self.across, self.blk = index, rows, columns, across, blk
        self.reach = REACH[index]
        self.ox = self.reach + 1
        self.nx = rows + 2 * self.ox + 2
        if across:
            self.cy = columns
            self.oy = 8
            self.ny = 8 + columns + 8
        else:
            self.cy = -(-(columns + 2 * self.reach) // 8) * 8
            self.oy = 8 + (self.cy - columns) // 2
            self.ny = self.cy + 16
        self.y = pl.ds(8, self.cy)
        self.own_x = pl.ds(self.ox, rows)
        self.own_y = pl.ds(self.oy, columns)
        self.half = 0.5 * 0.25**index

    def shape(self, *lead):
        return (*lead, self.nx, self.ny, 128)

    def span(self, radius):
        first = self.ox - radius
        count = self.rows + 2 * radius
        return first, -(-count // self.blk) * self.blk // self.blk


def overlap(size, step, radius):
    low = max(-radius, -step * size)
    high = min(size + radius, (1 - step) * size)
    return low + step * size, low, high - low


def kernel(sizes, levels, src_ref, tis_ref, dif_ref, upt_ref, out_ref, *scratch):
    gx_count, gy_count = sizes
    names = iter(scratch)
    tis = next(names)
    coef = [next(names) for _ in levels]
    right = [next(names) for _ in levels]
    kap = [next(names) for _ in levels]
    wgt = [next(names) for _ in levels]
    inv = [next(names) for _ in levels]
    dia = [next(names) for _ in levels]
    one = [next(names) for _ in levels]
    two = [next(names) for _ in levels]
    tri = [next(names) for _ in levels]
    gat_c, gat_b = next(names), next(names)
    local_sem, send_sem, recv_sem = next(names), next(names), next(names)

    gx = lax.axis_index("gx")
    gy = lax.axis_index("gy")
    parity = lax.rem(gx, 2)
    places = {}

    def device(dx, dy):
        if ("x", dx) not in places:
            places["x", dx] = lax.rem(gx + (dx + gx_count), gx_count) if dx else gx
        if ("y", dy) not in places:
            places["y", dy] = lax.rem(gy + (dy + gy_count), gy_count) if dy else gy
        return places["x", dx], places["y", dy]

    counter = [0]

    def remote(source, target, dx, dy):
        number = counter[0]
        counter[0] += 1
        copy = pltpu.make_async_remote_copy(
            src_ref=source,
            dst_ref=target,
            send_sem=send_sem.at[number],
            recv_sem=recv_sem.at[number],
            device_id=device(dx, dy),
            device_id_type=MESH,
        )
        copy.start()
        return copy

    def arrived(copies):
        for copy in copies:
            copy.wait_recv()

    def left(copies):
        for copy in copies:
            copy.wait_send()

    def around(level, radius):
        far = -(-radius // level.rows)
        return [(dx, dy) for dx in range(-far, far + 1) for dy in (-1, 0, 1) if (dx, dy) != (0, 0)]

    def send_block(ref, level, radius, lead=()):
        copies = []
        for dx, dy in around(level, radius):
            sx, tx, cx = overlap(level.rows, dx, radius)
            sy, ty, cy = overlap(level.columns, dy, radius)
            source = ref.at[(*lead, pl.ds(level.ox + sx, cx), pl.ds(level.oy + sy, cy))]
            target = ref.at[(*lead, pl.ds(level.ox + tx, cx), pl.ds(level.oy + ty, cy))]
            copies.append(remote(source, target, dx, dy))
        return copies

    def send_rows(ref, level, radius, lead=(), stride=1):
        copies = []
        far = -(-radius // level.rows)
        for step in range(1, far + 1):
            for dx in (step, -step):
                sx, tx, cx = overlap(level.rows, dx, radius)
                source = ref.at[(*lead, pl.ds(level.ox + sx, cx), level.y)]
                target = ref.at[(*lead, pl.ds(level.ox + tx, cx), level.y)]
                copies.append(remote(source, target, dx * stride, 0))
        return copies

    def send_columns(ref):
        return [remote(ref.at[gy], ref.at[gy], 0, dy) for dy in range(1, gy_count)]

    def loop(count, step):
        def body(i, carry):
            step(i)
            return carry

        lax.fori_loop(0, count, body, 0)

    def inside(level, x, blk, y, cy):
        base = gx // 2 if level.index == LEVELS - 1 else gx
        total = level.rows * (gx_count // 2 if level.index == LEVELS - 1 else gx_count)
        row = lax.broadcasted_iota(jnp.int32, (blk, cy, 128), 0) + (base * level.rows + x - level.ox)
        good = (row >= 0) & (row < total)
        if not level.across:
            column = lax.broadcasted_iota(jnp.int32, (blk, cy, 128), 1) + (gy * level.columns + y - level.oy)
            good = good & (column >= 0) & (column < level.columns * gy_count)
        return good

    def types(x, blk, y, cy, masked):
        zero = levels[0]
        kind = tis[pl.ds(x, blk), pl.ds(y, cy), :]
        kappa = jnp.full(kind.shape, dif_ref[0], F32)
        sigma = jnp.full(kind.shape, upt_ref[0], F32)
        for index in range(1, TYPES):
            hit = kind == index
            kappa = jnp.where(hit, dif_ref[index], kappa)
            sigma = jnp.where(hit, upt_ref[index], sigma)
        if masked:
            kappa = jnp.where(inside(zero, x, blk, y, cy), kappa, 0.0)
        kap[0][pl.ds(x, blk), pl.ds(y, cy), :] = kappa
        coef[0][pl.ds(x, blk), pl.ds(y, cy), :] = sigma

    def mean(ref, lead, x, y, count):
        even = pl.ds(y, count, stride=2)
        odd = pl.ds(y + 1, count, stride=2)
        near = ref[(*lead, x, even, slice(None))] + ref[(*lead, x + 1, even, slice(None))]
        far = ref[(*lead, x, odd, slice(None))] + ref[(*lead, x + 1, odd, slice(None))]
        return 0.25 * (near + far)

    def masked_kappa(level):
        index = level.index
        first, count = level.span(level.reach + 1)
        y, cy = (8, level.cy) if level.across else (7, level.cy + 2)

        def step(i):
            x = first + i * level.blk
            value = coef[index][0, pl.ds(x, level.blk), pl.ds(y, cy), :]
            value = jnp.where(inside(level, x, level.blk, y, cy), value, 0.0)
            kap[index][pl.ds(x, level.blk), pl.ds(y, cy), :] = value

        loop(count, step)

    def weights(level):
        index, blk, cy = level.index, level.blk, level.cy
        first, count = level.span(level.reach)
        field = kap[index]
        half = level.half

        def step(i):
            x = first + i * blk
            here = (pl.ds(x, blk), level.y, slice(None))
            centre = field[here]
            sigma = coef[index][here] if index == 0 else coef[index][(1, *here)]
            plane = lax.broadcasted_iota(jnp.int32, centre.shape, 2)
            top, bottom = plane == 127, plane == 0
            east = half * (centre + field[pl.ds(x + 1, blk), level.y, :])
            west = half * (centre + field[pl.ds(x - 1, blk), level.y, :])
            north = half * (centre + field[pl.ds(x, blk), pl.ds(9, cy), :])
            south = half * (centre + field[pl.ds(x, blk), pl.ds(7, cy), :])
            upper = HZ * (centre + jnp.where(top, 0.0, pltpu.roll(centre, 127, 2)))
            lower = HZ * (centre + jnp.where(bottom, 0.0, pltpu.roll(centre, 1, 2)))
            diag = east + west + north + south + upper + lower + sigma
            inverse = jnp.where(inside(level, x, blk, 8, cy), 0.8 / diag, 0.0)
            inv[index][here] = inverse
            dia[index][here] = 1.25 * diag
            out = wgt[index]
            out[(0, *here)] = inverse * east
            out[(1, *here)] = inverse * west
            out[(2, *here)] = inverse * north
            out[(3, *here)] = inverse * south
            out[(4, *here)] = jnp.where(top, 0.0, inverse * upper)
            out[(5, *here)] = jnp.where(bottom, 0.0, inverse * lower)

        loop(count, step)

    def pulled(level, field, x, blk, centre):
        index, cy = level.index, level.cy
        here = (pl.ds(x, blk), level.y, slice(None))
        weight = wgt[index]
        total = one[index][here] + weight[(0, *here)] * field[pl.ds(x + 1, blk), level.y, :]
        other = weight[(1, *here)] * field[pl.ds(x - 1, blk), level.y, :]
        total = total + weight[(2, *here)] * field[pl.ds(x, blk), pl.ds(9, cy), :]
        other = other + weight[(3, *here)] * field[pl.ds(x, blk), pl.ds(7, cy), :]
        total = total + weight[(4, *here)] * pltpu.roll(centre, 127, 2)
        other = other + weight[(5, *here)] * pltpu.roll(centre, 1, 2)
        return total + other

    def first_sweep(level):
        index, blk = level.index, level.blk
        first, count = level.span(level.reach)

        def step(i):
            here = (pl.ds(first + i * blk, blk), level.y, slice(None))
            one[index][here] = inv[index][here] * right[index][here]

        loop(count, step)

    def sweep(level, source, target, radius):
        blk = level.blk
        first, count = level.span(radius)

        def step(i):
            x = first + i * blk
            here = (pl.ds(x, blk), level.y, slice(None))
            centre = source[here]
            target[here] = 0.2 * centre + pulled(level, source, x, blk, centre)

        loop(count, step)

    def residual(level, radius):
        index, blk = level.index, level.blk
        first, count = level.span(radius)

        def step(i):
            x = first + i * blk
            here = (pl.ds(x, blk), level.y, slice(None))
            centre = two[index][here]
            total = pulled(level, two[index], x, blk, centre)
            tri[index][here] = dia[index][here] * (total - 0.8 * centre)

        loop(count, step)

    def lift(value, level, x, y, count):
        for row in (x, x + 1):
            for column in (y, y + 1):
                spot = (row, pl.ds(column, count, stride=2), slice(None))
                two[level.index][spot] = two[level.index][spot] + value

    zero, one_, two_, three, four, five = levels

    loads = []
    for position, (source, target) in enumerate(((tis_ref, tis), (src_ref, right[0]))):
        copy = pltpu.make_async_copy(source, target.at[zero.own_x, zero.own_y], local_sem.at[position])
        copy.start()
        loads.append(copy)
    barrier = pltpu.get_barrier_semaphore()
    greeted = around(two_, two_.reach + 1)
    greeted = greeted + [(0, dy) for dy in range(2, gy_count - 1)]
    for dx, dy in greeted:
        pl.semaphore_signal(barrier, inc=1, device_id=device(dx, dy), device_id_type=MESH)
    for level in (three, four, five):
        index = level.index
        for ref in (kap[index], one[index], two[index], tri[index]):
            ref[:, pl.ds(0, 8), :] = jnp.zeros((level.nx, 8, 128), F32)
            ref[:, pl.ds(8 + level.cy, 8), :] = jnp.zeros((level.nx, 8, 128), F32)
    loads[0].wait()
    loads[1].wait()
    pl.semaphore_wait(barrier, len(greeted))

    sent_tis = send_block(tis, zero, zero.reach + 1)
    sent_src = send_block(right[0], zero, zero.reach)
    loop(zero.rows // 2, lambda i: types(zero.ox + 2 * i, 2, zero.oy, zero.columns, False))

    def coarsen(ref, lead, fine, level, field):
        def step(i):
            value = mean(ref, lead, fine.ox + 2 * i, fine.oy, level.columns)
            coef[level.index][field, level.ox + i, level.own_y, :] = value

        loop(level.rows, step)

    coarsen(kap[0], (), zero, one_, 0)
    coarsen(coef[0], (), zero, one_, 1)
    sent_c1 = send_block(coef[1], one_, one_.reach + 1, (slice(None),))
    for field in (0, 1):
        coarsen(coef[1], (field,), one_, two_, field)
    sent_c2 = send_block(coef[2], two_, two_.reach + 1, (slice(None),))
    for field in (0, 1):
        for row in (0, 1):
            gat_c[gy, field, row] = mean(coef[2], (field,), two_.ox + 2 * row, two_.oy, 4)
    sent_c3 = send_columns(gat_c)

    arrived(sent_tis)
    ring = zero.reach + 1
    edges = ring // 2
    loop(edges, lambda i: types(zero.ox - ring + 2 * i, 2, 8, zero.cy, True))
    loop(edges, lambda i: types(zero.ox + zero.rows + 2 * i, 2, 8, zero.cy, True))
    loop(zero.rows // 4, lambda i: types(zero.ox + 4 * i, 4, 8, ring, True))
    loop(zero.rows // 4, lambda i: types(zero.ox + 4 * i, 4, zero.oy + zero.columns, ring, True))
    weights(zero)
    arrived(sent_src)

    def descend(level):
        index = level.index
        first_sweep(level)
        sweep(level, one[index], two[index], level.reach - 1)
        residual(level, 0)

    def restrict_to(fine, level):
        def step(i):
            value = mean(tri[fine.index], (), fine.ox + 2 * i, fine.oy, level.columns)
            right[level.index][level.ox + i, level.own_y, :] = value

        loop(level.rows, step)

    descend(zero)
    restrict_to(zero, one_)
    sent_b1 = send_block(right[1], one_, one_.reach)
    left(sent_tis)
    left(sent_src)
    arrived(sent_c1)
    masked_kappa(one_)
    weights(one_)

    arrived(sent_b1)
    descend(one_)
    restrict_to(one_, two_)
    sent_b2 = send_block(right[2], two_, two_.reach)
    arrived(sent_c2)
    masked_kappa(two_)
    weights(two_)
    arrived(sent_c3)

    def unpack(read, write):
        for part in range(gy_count):
            for row in (0, 1):
                write(row, pl.ds(8 + 4 * part, 4), read(part, row))

    for field in (0, 1):

        def write(row, columns, value):
            coef[3][field, three.ox + row, columns, :] = value

        unpack(lambda part, row: gat_c[part, field, row], write)
    sent_x3 = send_rows(coef[3], three, three.reach + 1, (slice(None),))
    for field in (0, 1):
        coef[4][field, four.ox, four.y, :] = mean(coef[3], (field,), three.ox, 8, four.cy)
    left(sent_c1)
    left(sent_c2)
    left(sent_c3)
    left(sent_b1)

    arrived(sent_b2)
    descend(two_)
    for row in (0, 1):
        gat_b[gy, row] = mean(tri[2], (), two_.ox + 2 * row, two_.oy, 4)
    sent_b3 = send_columns(gat_b)
    sent_c4 = send_rows(coef[4], four, four.reach + 1, (slice(None),))
    arrived(sent_x3)
    masked_kappa(three)
    weights(three)
    left(sent_b2)

    arrived(sent_b3)

    def write_right(row, columns, value):
        right[3][three.ox + row, columns, :] = value

    unpack(lambda part, row: gat_b[part, row], write_right)
    sent_r3 = send_rows(right[3], three, three.reach)
    arrived(sent_c4)
    chip = four.ox - parity
    for field in (0, 1):
        coef[5][field, five.ox, five.y, :] = mean(coef[4], (field,), chip, 8, five.cy)
    sent_c5 = send_rows(coef[5], five, five.reach + 1, (slice(None),), 2)
    masked_kappa(four)
    weights(four)
    left(sent_x3)
    left(sent_b3)
    left(sent_c4)
    arrived(sent_r3)
    descend(three)
    right[4][four.ox, four.y, :] = mean(tri[3], (), three.ox, 8, four.cy)

    sent_r4 = send_rows(right[4], four, four.reach)
    arrived(sent_c5)
    masked_kappa(five)
    weights(five)
    left(sent_r3)
    left(sent_c5)
    arrived(sent_r4)
    first_sweep(four)
    sweep(four, one[4], two[4], four.reach - 1)
    residual(four, 1)
    right[5][five.ox, five.y, :] = mean(tri[4], (), chip, 8, five.cy)

    sent_r5 = send_rows(right[5], five, five.reach, (), 2)
    left(sent_r4)
    arrived(sent_r5)
    first_sweep(five)
    sweep(five, one[5], two[5], 4)
    sweep(five, two[5], tri[5], 3)
    sweep(five, tri[5], two[5], 2)
    left(sent_r5)

    def ascend(level, last):
        index = level.index
        sweep(level, two[index], tri[index], last + 1)
        sweep(level, tri[index], two[index], last)

    for offset in range(-4, 5):
        row = five.ox - 4 + (parity + (offset + 8)) // 2
        value = two[5][row, five.y, :]
        for column in (8, 9):
            spot = (four.ox + offset, pl.ds(column, five.cy, stride=2), slice(None))
            two[4][spot] = two[4][spot] + value
    ascend(four, 2)
    for offset in range(-2, 3):
        lift(two[4][four.ox + offset, four.y, :], three, three.ox + 2 * offset, 8, four.cy)
    ascend(three, 2)
    for offset in range(-2, 4):
        value = two[3][three.ox + offset, pl.ds(6 + 4 * gy, 8), :]
        lift(value, two_, two_.ox + 2 * offset, two_.oy - 4, 8)
    ascend(two_, 2)

    def lift_one(i):
        value = two[2][two_.ox - 2 + i, pl.ds(two_.oy - 2, two_.columns + 4), :]
        lift(value, one_, one_.ox - 4 + 2 * i, one_.oy - 4, two_.columns + 4)

    loop(two_.rows + 4, lift_one)
    ascend(one_, 1)

    def lift_zero(i):
        value = two[1][one_.ox - 1 + i, pl.ds(one_.oy - 1, one_.columns + 2), :]
        lift(value, zero, zero.ox - 2 + 2 * i, zero.oy - 2, one_.columns + 2)

    loop(one_.rows + 2, lift_zero)
    ascend(zero, 0)

    def store(i):
        out_ref[pl.ds(2 * i, 2)] = two[0][pl.ds(zero.ox + 2 * i, 2), zero.own_y, :]

    loop(zero.rows // 2, store)


def build(mesh, rows, columns):
    gx_count, gy_count = mesh.shape["gx"], mesh.shape["gy"]
    levels = [
        Level(0, rows, columns, False, 2),
        Level(1, rows // 2, columns // 2, False, 2),
        Level(2, rows // 4, columns // 4, False, 2),
        Level(3, rows // 8, columns // 8 * gy_count, True, 2),
        Level(4, rows // 16, columns // 16 * gy_count, True, 3),
        Level(5, 1, columns // 32 * gy_count, True, 3),
    ]
    zero = levels[0]
    messages = 160
    scratch = [pltpu.VMEM(zero.shape(), jnp.int32)]
    scratch += [pltpu.VMEM(level.shape(2) if level.index else level.shape(), F32) for level in levels]
    scratch += [pltpu.VMEM(level.shape(), F32) for level in levels]
    scratch += [pltpu.VMEM(level.shape(), F32) for level in levels]
    scratch += [pltpu.VMEM(level.shape(6), F32) for level in levels]
    for _ in range(5):
        scratch += [pltpu.VMEM(level.shape(), F32) for level in levels]
    scratch += [
        pltpu.VMEM((gy_count, 2, 2, 4, 128), F32),
        pltpu.VMEM((gy_count, 2, 4, 128), F32),
        pltpu.SemaphoreType.DMA((2,)),
        pltpu.SemaphoreType.DMA((messages,)),
        pltpu.SemaphoreType.DMA((messages,)),
    ]
    return pl.pallas_call(
        functools.partial(kernel, (gx_count, gy_count), levels),
        out_shape=jax.ShapeDtypeStruct((rows, columns, 128), F32),
        in_specs=[
            pl.BlockSpec(memory_space=pl.ANY),
            pl.BlockSpec(memory_space=pl.ANY),
            pl.BlockSpec(memory_space=pltpu.SMEM),
            pl.BlockSpec(memory_space=pltpu.SMEM),
        ],
        out_specs=pl.BlockSpec(memory_space=pltpu.VMEM),
        scratch_shapes=scratch,
        name="vcycle",
        compiler_params=pltpu.CompilerParams(
            collective_id=0, has_side_effects=True, vmem_limit_bytes=40 * 2**20
        ),
    )


def solution(mesh):
    def body(source, tissue, diffusivity, uptake):
        call = build(mesh, source.shape[0], source.shape[1])
        return call(source, tissue, diffusivity, uptake)

    in_specs = (P("gx", "gy", None), P("gx", "gy", None), P(), P())
    out_specs = P("gx", "gy", None)
    return jax.shard_map(body, mesh=mesh, in_specs=in_specs, out_specs=out_specs, check_vma=False)
```

```python
import functools

import jax
import jax.numpy as jnp
from jax import lax
from jax.experimental import pallas as pl
from jax.experimental.pallas import tpu as pltpu
from jax.sharding import PartitionSpec as P

MESH = pl.DeviceIdType.MESH
F32 = jnp.float32
LEVELS = 6
TYPES = 8
HZ = 0.5 * 0.015625
REACH = (3, 4, 5, 5, 5, 5)


class Level:
    def __init__(self, index, rows, columns, across, most):
        self.index, self.rows, self.columns, self.across, self.most = index, rows, columns, across, most
        self.reach = REACH[index]
        self.ox = self.reach + 1
        self.nx = rows + 2 * self.ox + 2
        if across:
            self.oy = 8
            self.wide = self.mid = self.core = (8, columns)
            self.ny = 8 + columns + 8
        else:
            self.oy = 12
            self.core = (12, columns)
            around = -(-(columns + 8) // 8) * 8
            self.mid = (8, around)
            self.wide = (8, around) if self.reach < 5 else (4, around + 8)
            self.ny = around + 16
        self.own_x = pl.ds(self.ox, rows)
        self.own_y = pl.ds(self.oy, columns)
        self.half = 0.5 * 0.25**index

    def shape(self, *lead):
        return (*lead, self.nx, self.ny, 128)

    def span(self, radius):
        count = self.rows + 2 * radius
        times = -(-count // self.most)
        return self.ox - radius, -(-count // times), times


def overlap(size, step, radius, known):
    if known:
        low, high = {1: (-radius, -known), 0: (-known, size + known), -1: (size + known, size + radius)}[step]
        return low + step * size, low, high - low
    low = max(-radius, -step * size)
    high = min(size + radius, (1 - step) * size)
    return low + step * size, low, high - low


def kernel(sizes, levels, src_ref, tis_ref, dif_ref, upt_ref, out_ref, *scratch):
    gx_count, gy_count = sizes
    names = iter(scratch)
    tis = next(names)
    coef = [next(names) for _ in levels]
    right = [next(names) for _ in levels]
    wgt = [next(names) for _ in levels]
    inv = [next(names) for _ in levels]
    dia = [next(names) for _ in levels]
    one = [next(names) for _ in levels]
    two = [next(names) for _ in levels]
    tri = [next(names) for _ in levels]
    gat_c, gat_b = next(names), next(names)
    dif, upt = next(names), next(names)
    local_sem, send_sem, recv_sem = next(names), next(names), next(names)

    gx = lax.axis_index("gx")
    gy = lax.axis_index("gy")
    parity = lax.rem(gx, 2)
    places = {}

    def device(dx, dy):
        if ("x", dx) not in places:
            places["x", dx] = lax.rem(gx + (dx + gx_count), gx_count) if dx else gx
        if ("y", dy) not in places:
            places["y", dy] = lax.rem(gy + (dy + gy_count), gy_count) if dy else gy
        return places["x", dx], places["y", dy]

    counter = [0]

    def remote(source, target, dx, dy):
        number = counter[0]
        counter[0] += 1
        copy = pltpu.make_async_remote_copy(
            src_ref=source,
            dst_ref=target,
            send_sem=send_sem.at[number],
            recv_sem=recv_sem.at[number],
            device_id=device(dx, dy),
            device_id_type=MESH,
        )
        copy.start()
        return copy

    def arrived(copies):
        for copy in copies:
            copy.wait_recv()

    def left(copies):
        for copy in copies:
            copy.wait_send()

    def around(level, radius, known=0):
        far = -(-(radius - known) // level.rows)
        return [(dx, dy) for dx in range(-far, far + 1) for dy in (-1, 0, 1) if (dx, dy) != (0, 0)]

    def send_block(ref, level, radius, lead=(), known=0):
        copies = []
        for dx, dy in sorted(around(level, radius, known), key=lambda step: -abs(step[0]) - abs(step[1])):
            sx, tx, cx = overlap(level.rows, dx, radius, known)
            sy, ty, cy = overlap(level.columns, dy, radius, known)
            source = ref.at[(*lead, pl.ds(level.ox + sx, cx), pl.ds(level.oy + sy, cy))]
            target = ref.at[(*lead, pl.ds(level.ox + tx, cx), pl.ds(level.oy + ty, cy))]
            copies.append(remote(source, target, dx, dy))
        return copies

    def send_rows(ref, level, radius, lead=(), stride=1):
        copies = []
        far = -(-radius // level.rows)
        for step in range(1, far + 1):
            for dx in (step, -step):
                sx, tx, cx = overlap(level.rows, dx, radius, 0)
                source = ref.at[(*lead, pl.ds(level.ox + sx, cx), level.own_y)]
                target = ref.at[(*lead, pl.ds(level.ox + tx, cx), level.own_y)]
                copies.append(remote(source, target, dx * stride, 0))
        return copies

    def send_known(ref, level, moves, stride=1):
        copies = []
        for step, sx, tx, cx in moves:
            source = ref.at[pl.ds(level.ox + sx, cx), level.own_y]
            target = ref.at[pl.ds(level.ox + tx, cx), level.own_y]
            copies.append(remote(source, target, step * stride, 0))
        return copies

    def send_columns(ref):
        return [remote(ref.at[gy], ref.at[gy], 0, dy) for dy in range(1, gy_count)]

    def loop(count, step):
        def body(i, carry):
            step(i)
            return carry

        lax.fori_loop(0, count, body, 0)

    def seam(level, shape, axis, start, last):
        if axis == 0:
            half = level.index == LEVELS - 1
            total = level.rows * (gx_count // 2 if half else gx_count)
            base = (gx // 2 if half else gx) * level.rows + start - level.ox
        else:
            total = level.columns * gy_count
            base = gy * level.columns + start - level.oy
        place = lax.broadcasted_iota(jnp.int32, shape, axis) + base
        if last:
            return (place == total - 1) | (place == -1)
        return (place == 0) | (place == total)

    def types(x, blk, y, cy):
        kind = tis[pl.ds(x, blk), pl.ds(y, cy), :]
        kappa = jnp.full(kind.shape, dif[0], F32)
        sigma = jnp.full(kind.shape, upt[0], F32)
        for index in range(1, TYPES):
            hit = kind == index
            kappa = jnp.where(hit, dif[index], kappa)
            sigma = jnp.where(hit, upt[index], sigma)
        coef[0][0, pl.ds(x, blk), pl.ds(y, cy), :] = kappa
        coef[0][1, pl.ds(x, blk), pl.ds(y, cy), :] = sigma

    def mean(ref, lead, x, y, count):
        even = pl.ds(y, count, stride=2)
        odd = pl.ds(y + 1, count, stride=2)
        near = ref[(*lead, x, even, slice(None))] + ref[(*lead, x + 1, even, slice(None))]
        far = ref[(*lead, x, odd, slice(None))] + ref[(*lead, x + 1, odd, slice(None))]
        return 0.25 * (near + far)

    def weights(level, rows=None, columns=None, start=False):
        index = level.index
        first, blk, times = rows or level.span(level.reach)
        y, cy = columns or level.wide
        half = level.half

        def step(i):
            x = first + i * blk
            here = (pl.ds(x, blk), pl.ds(y, cy), slice(None))
            field = coef[index].at[0]
            centre = field[here]
            plane = lax.broadcasted_iota(jnp.int32, centre.shape, 2)
            row, column = pl.ds(x, blk), pl.ds(y, cy)
            faces = [
                (half, field[pl.ds(x + 1, blk), column, :], seam(level, centre.shape, 0, x, True)),
                (half, field[pl.ds(x - 1, blk), column, :], seam(level, centre.shape, 0, x, False)),
            ]
            if level.across:
                faces += [
                    (half, field[row, pl.ds(y + 1, cy), :], None),
                    (half, field[row, pl.ds(y - 1, cy), :], None),
                ]
            else:
                faces += [
                    (half, field[row, pl.ds(y + 1, cy), :], seam(level, centre.shape, 1, y, True)),
                    (half, field[row, pl.ds(y - 1, cy), :], seam(level, centre.shape, 1, y, False)),
                ]
            faces += [
                (HZ, pltpu.roll(centre, 127, 2), plane == 127),
                (HZ, pltpu.roll(centre, 1, 2), plane == 0),
            ]
            diag = coef[index][(1, *here)]
            weight = []
            for scale, beyond, closed in faces:
                if closed is not None:
                    beyond = jnp.where(closed, 0.0, beyond)
                face = scale * (centre + beyond)
                diag = diag + face
                weight.append(face)
            inverse = 0.8 / diag
            dia[index][here] = 1.25 * diag
            if start:
                one[index][here] = inverse * right[index][here]
            else:
                inv[index][here] = inverse
            for number, (scale, beyond, closed) in enumerate(faces):
                value = inverse * weight[number]
                if closed is not None:
                    value = jnp.where(closed, 0.0, value)
                wgt[index][(number, *here)] = value

        loop(times, step)

    def pulled(level, field, x, blk, y, cy, centre):
        index = level.index
        here = (pl.ds(x, blk), pl.ds(y, cy), slice(None))
        weight = wgt[index]
        total = one[index][here] + weight[(0, *here)] * field[pl.ds(x + 1, blk), pl.ds(y, cy), :]
        other = weight[(1, *here)] * field[pl.ds(x - 1, blk), pl.ds(y, cy), :]
        total = total + weight[(2, *here)] * field[pl.ds(x, blk), pl.ds(y + 1, cy), :]
        other = other + weight[(3, *here)] * field[pl.ds(x, blk), pl.ds(y - 1, cy), :]
        total = total + weight[(4, *here)] * pltpu.roll(centre, 127, 2)
        other = other + weight[(5, *here)] * pltpu.roll(centre, 1, 2)
        return total + other

    def first_sweep(level):
        index = level.index
        first, blk, times = level.span(level.reach)

        def step(i):
            here = (pl.ds(first + i * blk, blk), pl.ds(*level.wide), slice(None))
            one[index][here] = inv[index][here] * right[index][here]

        loop(times, step)

    def sweep(level, source, target, radius):
        first, blk, times = level.span(radius)
        y, cy = level.mid if radius else level.core

        def step(i):
            x = first + i * blk
            here = (pl.ds(x, blk), pl.ds(y, cy), slice(None))
            centre = source[here]
            target[here] = 0.2 * centre + pulled(level, source, x, blk, y, cy, centre)

        loop(times, step)

    def residual(level, radius, columns):
        index = level.index
        first, blk, times = level.span(radius)
        y, cy = columns

        def step(i):
            x = first + i * blk
            here = (pl.ds(x, blk), pl.ds(y, cy), slice(None))
            centre = two[index][here]
            total = pulled(level, two[index], x, blk, y, cy, centre)
            tri[index][here] = dia[index][here] * (total - 0.8 * centre)

        loop(times, step)

    def lift(value, level, x, y, count):
        for row in (x, x + 1):
            for column in (y, y + 1):
                spot = (row, pl.ds(column, count, stride=2), slice(None))
                two[level.index][spot] = two[level.index][spot] + value

    zero, one_, two_, three, four, five = levels

    loads = []
    for position, (source, target) in enumerate(
        (
            (tis_ref, tis.at[zero.own_x, zero.own_y]),
            (src_ref, right[0].at[zero.own_x, zero.own_y]),
            (dif_ref, dif),
            (upt_ref, upt),
        )
    ):
        copy = pltpu.make_async_copy(source, target, local_sem.at[position])
        copy.start()
        loads.append(copy)
    barrier = pltpu.get_barrier_semaphore()
    greeted = around(two_, two_.reach + 1)
    greeted = greeted + [(0, dy) for dy in range(2, gy_count - 1)]
    for dx, dy in greeted:
        pl.semaphore_signal(barrier, inc=1, device_id=device(dx, dy), device_id_type=MESH)
    for level in (three, four, five):
        index = level.index
        for ref in (coef[index].at[0], one[index], two[index], tri[index]):
            ref[:, pl.ds(0, 8), :] = jnp.zeros((level.nx, 8, 128), F32)
            ref[:, pl.ds(8 + level.columns, 8), :] = jnp.zeros((level.nx, 8, 128), F32)
    for copy in loads:
        copy.wait()
    pl.semaphore_wait(barrier, len(greeted))

    sent_tis = send_block(tis, zero, zero.reach + 1)
    sent_src = send_block(right[0], zero, zero.reach)
    loop(zero.rows // 2, lambda i: types(zero.ox + 2 * i, 2, zero.oy, zero.columns))

    def coarsen(ref, lead, fine, level, field):
        def step(i):
            value = mean(ref, lead, fine.ox + 2 * i, fine.oy, level.columns)
            coef[level.index][field, level.ox + i, level.own_y, :] = value

        loop(level.rows, step)

    coarsen(coef[0], (0,), zero, one_, 0)
    coarsen(coef[0], (1,), zero, one_, 1)
    sent_c1 = send_block(coef[1], one_, one_.reach + 1, (slice(None),))
    for field in (0, 1):
        coarsen(coef[1], (field,), one_, two_, field)
    sent_c2 = send_block(coef[2], two_, two_.reach + 1, (slice(None),))
    for field in (0, 1):
        for row in (0, 1):
            gat_c[gy, field, row] = mean(coef[2], (field,), two_.ox + 2 * row, two_.oy, 4)
    sent_c3 = send_columns(gat_c)
    weights(zero, (zero.ox + 1, (zero.rows - 2) // 2, 2), zero.core, True)

    arrived(sent_tis)
    ring = zero.reach + 1
    types(zero.ox - ring, ring, 8, zero.mid[1])
    types(zero.ox + zero.rows, ring, 8, zero.mid[1])
    loop(zero.rows // 8, lambda i: types(zero.ox + 8 * i, 8, 8, ring))
    loop(zero.rows // 8, lambda i: types(zero.ox + 8 * i, 8, zero.oy + zero.columns, ring))
    arrived(sent_src)
    weights(zero, (zero.ox - zero.reach, zero.reach + 1, 1), zero.wide, True)
    weights(zero, (zero.ox + zero.rows - 1, zero.reach + 1, 1), zero.wide, True)
    weights(zero, (zero.ox + 1, (zero.rows - 2) // 2, 2), (8, 8), True)
    weights(zero, (zero.ox + 1, (zero.rows - 2) // 2, 2), (zero.oy + zero.columns - 4, 8), True)

    def restrict_to(fine, level, known):
        def step(i):
            value = mean(tri[fine.index], (), fine.ox + 2 * (i - known), fine.oy - 2 * known, level.columns + 2 * known)
            right[level.index][level.ox - known + i, pl.ds(level.oy - known, level.columns + 2 * known), :] = value

        loop(level.rows + 2 * known, step)

    sweep(zero, one[0], two[0], zero.reach - 1)
    residual(zero, 0, zero.core)
    restrict_to(zero, one_, 0)
    sent_b1 = send_block(right[1], one_, one_.reach)
    left(sent_tis)
    left(sent_src)
    arrived(sent_c1)
    weights(one_)

    arrived(sent_b1)
    first_sweep(one_)
    sweep(one_, one[1], two[1], one_.reach - 1)
    residual(one_, 2, one_.mid)
    restrict_to(one_, two_, 1)
    sent_b2 = send_block(right[2], two_, two_.reach, (), 1)
    arrived(sent_c2)
    weights(two_)
    arrived(sent_c3)

    def unpack(rows, read, write):
        for part in range(gy_count):
            for row in range(rows):
                write(row, pl.ds(8 + 4 * part, 4), read(part, row))

    for field in (0, 1):

        def write(row, columns, value):
            coef[3][field, three.ox + row, columns, :] = value

        unpack(2, lambda part, row: gat_c[part, field, row], write)
    sent_x3 = send_rows(coef[3], three, three.reach + 1, (slice(None),))
    for field in (0, 1):
        coef[4][field, four.ox, four.own_y, :] = mean(coef[3], (field,), three.ox, 8, four.columns)
    left(sent_c1)
    left(sent_c2)
    left(sent_c3)
    left(sent_b1)

    arrived(sent_b2)
    first_sweep(two_)
    sweep(two_, one[2], two[2], two_.reach - 1)
    residual(two_, 2, two_.core)
    for row in range(4):
        gat_b[gy, row] = mean(tri[2], (), two_.ox - 2 + 2 * row, two_.oy, 4)
    sent_b3 = send_columns(gat_b)
    arrived(sent_x3)
    sent_c4 = send_rows(coef[4], four, four.reach + 1, (slice(None),))
    weights(three)
    left(sent_b2)

    arrived(sent_b3)

    def write_right(row, columns, value):
        right[3][three.ox - 1 + row, columns, :] = value

    unpack(4, lambda part, row: gat_b[part, row], write_right)
    sent_r3 = send_known(right[3], three, ((2, -1, -5, 4), (-2, -1, 3, 4)))
    arrived(sent_c4)
    chip = four.ox - parity
    for field in (0, 1):
        coef[5][field, five.ox, five.own_y, :] = mean(coef[4], (field,), chip, 8, five.columns)
    sent_c5 = send_rows(coef[5], five, five.reach + 1, (slice(None),), 2)
    weights(four)
    left(sent_x3)
    left(sent_b3)
    left(sent_c4)
    arrived(sent_r3)
    first_sweep(three)
    sweep(three, one[3], two[3], three.reach - 1)
    residual(three, 2, three.core)
    for row in (-1, 0, 1):
        right[4][four.ox + row, four.own_y, :] = mean(tri[3], (), three.ox + 2 * row, 8, four.columns)

    moves = ((4, -1, -5, 1), (-4, 1, 5, 1), (3, -1, -4, 3), (-3, -1, 2, 3))
    sent_r4 = send_known(right[4], four, moves)
    arrived(sent_c5)
    weights(five)
    left(sent_r3)
    left(sent_c5)
    arrived(sent_r4)
    first_sweep(four)
    sweep(four, one[4], two[4], four.reach - 1)
    residual(four, 3, four.core)
    for row in (-1, 0, 1):
        right[5][five.ox + row, five.own_y, :] = mean(tri[4], (), chip + 2 * row, 8, five.columns)

    sent_r5 = send_known(right[5], five, moves, 2)
    left(sent_r4)
    arrived(sent_r5)
    first_sweep(five)
    sweep(five, one[5], two[5], 4)
    sweep(five, two[5], tri[5], 3)
    sweep(five, tri[5], two[5], 2)
    left(sent_r5)

    def ascend(level, last):
        index = level.index
        sweep(level, two[index], tri[index], last + 1)
        sweep(level, tri[index], two[index], last)

    for offset in range(-4, 5):
        row = five.ox - 4 + (parity + (offset + 8)) // 2
        value = two[5][row, five.own_y, :]
        for column in (8, 9):
            spot = (four.ox + offset, pl.ds(column, five.columns, stride=2), slice(None))
            two[4][spot] = two[4][spot] + value
    ascend(four, 2)
    for offset in range(-2, 3):
        lift(two[4][four.ox + offset, four.own_y, :], three, three.ox + 2 * offset, 8, four.columns)
    ascend(three, 2)
    for offset in range(-2, 4):
        value = two[3][three.ox + offset, pl.ds(6 + 4 * gy, 8), :]
        lift(value, two_, two_.ox + 2 * offset, two_.oy - 4, 8)
    ascend(two_, 2)

    def lift_one(i):
        value = two[2][two_.ox - 2 + i, pl.ds(two_.oy - 2, two_.columns + 4), :]
        lift(value, one_, one_.ox - 4 + 2 * i, one_.oy - 4, two_.columns + 4)

    loop(two_.rows + 4, lift_one)
    ascend(one_, 1)

    def lift_zero(i):
        value = two[1][one_.ox - 1 + i, pl.ds(one_.oy - 1, one_.columns + 2), :]
        lift(value, zero, zero.ox - 2 + 2 * i, zero.oy - 2, one_.columns + 2)

    loop(one_.rows + 2, lift_zero)
    sweep(zero, two[0], tri[0], 1)
    y, cy = zero.core
    part = zero.rows // 4
    copies = []
    for chunk in range(4):
        x = zero.ox + chunk * part
        here = (pl.ds(x, part), pl.ds(y, cy), slice(None))
        centre = tri[0][here]
        two[0][here] = 0.2 * centre + pulled(zero, tri[0], x, part, y, cy, centre)
        copy = pltpu.make_async_copy(
            two[0].at[pl.ds(x, part), pl.ds(y, cy)], out_ref.at[pl.ds(chunk * part, part)], local_sem.at[chunk]
        )
        copy.start()
        copies.append(copy)
    for copy in copies:
        copy.wait()


def build(mesh, rows, columns):
    gx_count, gy_count = mesh.shape["gx"], mesh.shape["gy"]
    levels = [
        Level(0, rows, columns, False, 5),
        Level(1, rows // 2, columns // 2, False, 7),
        Level(2, rows // 4, columns // 4, False, 12),
        Level(3, rows // 8, columns // 8 * gy_count, True, 6),
        Level(4, rows // 16, columns // 16 * gy_count, True, 11),
        Level(5, 1, columns // 32 * gy_count, True, 11),
    ]
    zero = levels[0]
    messages = 160
    scratch = [pltpu.VMEM(zero.shape(), jnp.int32)]
    scratch += [pltpu.VMEM(level.shape(2), F32) for level in levels]
    scratch += [pltpu.VMEM(level.shape(), F32) for level in levels]
    scratch += [pltpu.VMEM(level.shape(6), F32) for level in levels]
    for _ in range(5):
        scratch += [pltpu.VMEM(level.shape(), F32) for level in levels]
    scratch += [
        pltpu.VMEM((gy_count, 2, 2, 4, 128), F32),
        pltpu.VMEM((gy_count, 4, 4, 128), F32),
        pltpu.SMEM((TYPES,), F32),
        pltpu.SMEM((TYPES,), F32),
        pltpu.SemaphoreType.DMA((4,)),
        pltpu.SemaphoreType.DMA((messages,)),
        pltpu.SemaphoreType.DMA((messages,)),
    ]
    return pl.pallas_call(
        functools.partial(kernel, (gx_count, gy_count), levels),
        out_shape=jax.ShapeDtypeStruct((rows, columns, 128), F32),
        in_specs=[
            pl.BlockSpec(memory_space=pltpu.HBM),
            pl.BlockSpec(memory_space=pltpu.HBM),
            pl.BlockSpec(memory_space=pltpu.HBM),
            pl.BlockSpec(memory_space=pltpu.HBM),
        ],
        out_specs=pl.BlockSpec(memory_space=pltpu.HBM),
        scratch_shapes=scratch,
        name="vcycle",
        compiler_params=pltpu.CompilerParams(
            collective_id=0, has_side_effects=True, vmem_limit_bytes=64 * 2**20
        ),
    )


def solution(mesh):
    def body(source, tissue, diffusivity, uptake):
        call = build(mesh, source.shape[0], source.shape[1])
        return call(source, tissue, diffusivity, uptake)

    in_specs = (P("gx", "gy", None), P("gx", "gy", None), P(), P())
    out_specs = P("gx", "gy", None)
    return jax.shard_map(body, mesh=mesh, in_specs=in_specs, out_specs=out_specs, check_vma=False)
```

```python
import functools

import jax
import jax.numpy as jnp
from jax import lax
from jax.experimental import pallas as pl
from jax.experimental.pallas import tpu as pltpu
from jax.sharding import PartitionSpec as P

MESH = pl.DeviceIdType.MESH
F32 = jnp.float32
LEVELS = 6
TYPES = 8
HZ = 0.5 * 0.015625
REACH = (3, 4, 5, 5, 5, 5)


class Level:
    def __init__(self, index, rows, columns, across, most):
        self.index, self.rows, self.columns, self.across, self.most = index, rows, columns, across, most
        self.reach = REACH[index]
        self.ox = self.reach + 1
        self.nx = rows + 2 * self.ox + 2
        if across:
            self.oy = 8
            self.wide = self.mid = self.core = (8, columns)
            self.ny = 8 + columns + 8
        else:
            self.oy = 12
            self.core = (12, columns)
            around = -(-(columns + 8) // 8) * 8
            self.mid = (8, around)
            self.wide = (8, around) if self.reach < 5 else (4, around + 8)
            self.ny = around + 16
        self.own_x = pl.ds(self.ox, rows)
        self.own_y = pl.ds(self.oy, columns)
        self.half = 0.5 * 0.25**index

    def shape(self, *lead):
        return (*lead, self.nx, self.ny, 128)

    def span(self, radius):
        count = self.rows + 2 * radius
        times = -(-count // self.most)
        return self.ox - radius, -(-count // times), times


def overlap(size, step, radius, known):
    if known:
        low, high = {1: (-radius, -known), 0: (-known, size + known), -1: (size + known, size + radius)}[step]
        return low + step * size, low, high - low
    low = max(-radius, -step * size)
    high = min(size + radius, (1 - step) * size)
    return low + step * size, low, high - low


def kernel(sizes, levels, src_ref, tis_ref, dif_ref, upt_ref, out_ref, *scratch):
    gx_count, gy_count = sizes
    names = iter(scratch)
    tis = next(names)
    coef = [next(names) for _ in levels]
    right = [next(names) for _ in levels]
    wgt = [next(names) for _ in levels]
    inv = [next(names) for _ in levels]
    dia = [next(names) for _ in levels]
    one = [next(names) for _ in levels]
    two = [next(names) for _ in levels]
    tri = [next(names) for _ in levels]
    gat_c, gat_b = next(names), next(names)
    dif, upt = next(names), next(names)
    local_sem, send_sem, recv_sem = next(names), next(names), next(names)

    gx = lax.axis_index("gx")
    gy = lax.axis_index("gy")
    parity = lax.rem(gx, 2)
    places = {}

    def device(dx, dy):
        if ("x", dx) not in places:
            places["x", dx] = lax.rem(gx + (dx + gx_count), gx_count) if dx else gx
        if ("y", dy) not in places:
            places["y", dy] = lax.rem(gy + (dy + gy_count), gy_count) if dy else gy
        return places["x", dx], places["y", dy]

    counter = [0]

    def remote(source, target, dx, dy):
        number = counter[0]
        counter[0] += 1
        copy = pltpu.make_async_remote_copy(
            src_ref=source,
            dst_ref=target,
            send_sem=send_sem.at[number],
            recv_sem=recv_sem.at[number],
            device_id=device(dx, dy),
            device_id_type=MESH,
        )
        copy.start()
        return copy

    def arrived(copies):
        for copy in copies:
            copy.wait_recv()

    def left(copies):
        for copy in copies:
            copy.wait_send()

    def around(level, radius, known=0):
        far = -(-(radius - known) // level.rows)
        return [(dx, dy) for dx in range(-far, far + 1) for dy in (-1, 0, 1) if (dx, dy) != (0, 0)]

    def send_block(ref, level, radius, lead=(), known=0, origin=None):
        copies = []
        for dx, dy in sorted(around(level, radius, known), key=lambda step: -abs(step[0]) - abs(step[1])):
            sx, tx, cx = overlap(level.rows, dx, radius, known)
            sy, ty, cy = overlap(level.columns, dy, radius, known)
            if origin is None:
                source = ref.at[(*lead, pl.ds(level.ox + sx, cx), pl.ds(level.oy + sy, cy))]
            else:
                source = origin.at[pl.ds(sx, cx), pl.ds(sy, cy)]
            target = ref.at[(*lead, pl.ds(level.ox + tx, cx), pl.ds(level.oy + ty, cy))]
            copies.append(remote(source, target, dx, dy))
        return copies

    def send_known(ref, level, moves, stride=1, lead=()):
        copies = []
        for step, sx, tx, cx in moves:
            source = ref.at[(*lead, pl.ds(level.ox + sx, cx), level.own_y)]
            target = ref.at[(*lead, pl.ds(level.ox + tx, cx), level.own_y)]
            copies.append(remote(source, target, step * stride, 0))
        return copies

    def send_columns(ref):
        return [remote(ref.at[gy], ref.at[gy], 0, dy) for dy in range(1, gy_count)]

    def loop(count, step):
        def body(i, carry):
            step(i)
            return carry

        lax.fori_loop(0, count, body, 0)

    def seam(level, shape, axis, start, last):
        if axis == 0:
            half = level.index == LEVELS - 1
            total = level.rows * (gx_count // 2 if half else gx_count)
            base = (gx // 2 if half else gx) * level.rows + start - level.ox
        else:
            total = level.columns * gy_count
            base = gy * level.columns + start - level.oy
        place = lax.broadcasted_iota(jnp.int32, shape, axis) + base
        if last:
            return (place == total - 1) | (place == -1)
        return (place == 0) | (place == total)

    def types(x, blk, y, cy):
        kind = tis[pl.ds(x, blk), pl.ds(y, cy), :]
        kappa = jnp.full(kind.shape, dif[0], F32)
        sigma = jnp.full(kind.shape, upt[0], F32)
        for index in range(1, TYPES):
            hit = kind == index
            kappa = jnp.where(hit, dif[index], kappa)
            sigma = jnp.where(hit, upt[index], sigma)
        coef[0][0, pl.ds(x, blk), pl.ds(y, cy), :] = kappa
        coef[0][1, pl.ds(x, blk), pl.ds(y, cy), :] = sigma

    def mean(ref, lead, x, y, count):
        even = pl.ds(y, count, stride=2)
        odd = pl.ds(y + 1, count, stride=2)
        near = ref[(*lead, x, even, slice(None))] + ref[(*lead, x + 1, even, slice(None))]
        far = ref[(*lead, x, odd, slice(None))] + ref[(*lead, x + 1, odd, slice(None))]
        return 0.25 * (near + far)

    def weights(level, rows=None, columns=None, start=False):
        index = level.index
        first, blk, times = rows or level.span(level.reach)
        y, cy = columns or level.wide
        half = level.half

        def step(i):
            x = first + i * blk
            here = (pl.ds(x, blk), pl.ds(y, cy), slice(None))
            field = coef[index].at[0]
            centre = field[here]
            plane = lax.broadcasted_iota(jnp.int32, centre.shape, 2)
            row, column = pl.ds(x, blk), pl.ds(y, cy)
            faces = [
                (half, field[pl.ds(x + 1, blk), column, :], seam(level, centre.shape, 0, x, True)),
                (half, field[pl.ds(x - 1, blk), column, :], seam(level, centre.shape, 0, x, False)),
            ]
            if level.across:
                faces += [
                    (half, field[row, pl.ds(y + 1, cy), :], None),
                    (half, field[row, pl.ds(y - 1, cy), :], None),
                ]
            else:
                faces += [
                    (half, field[row, pl.ds(y + 1, cy), :], seam(level, centre.shape, 1, y, True)),
                    (half, field[row, pl.ds(y - 1, cy), :], seam(level, centre.shape, 1, y, False)),
                ]
            faces += [
                (HZ, pltpu.roll(centre, 127, 2), plane == 127),
                (HZ, pltpu.roll(centre, 1, 2), plane == 0),
            ]
            diag = coef[index][(1, *here)]
            weight = []
            for scale, beyond, closed in faces:
                if closed is not None:
                    beyond = jnp.where(closed, 0.0, beyond)
                face = scale * (centre + beyond)
                diag = diag + face
                weight.append(face)
            inverse = 0.8 / diag
            dia[index][here] = 1.25 * diag
            if start:
                one[index][here] = inverse * right[index][here]
            else:
                inv[index][here] = inverse
            for number, (scale, beyond, closed) in enumerate(faces):
                value = inverse * weight[number]
                if closed is not None:
                    value = jnp.where(closed, 0.0, value)
                wgt[index][(number, *here)] = value

        loop(times, step)

    def pulled(level, field, x, blk, y, cy, centre):
        index = level.index
        here = (pl.ds(x, blk), pl.ds(y, cy), slice(None))
        weight = wgt[index]
        total = one[index][here] + weight[(0, *here)] * field[pl.ds(x + 1, blk), pl.ds(y, cy), :]
        other = weight[(1, *here)] * field[pl.ds(x - 1, blk), pl.ds(y, cy), :]
        total = total + weight[(2, *here)] * field[pl.ds(x, blk), pl.ds(y + 1, cy), :]
        other = other + weight[(3, *here)] * field[pl.ds(x, blk), pl.ds(y - 1, cy), :]
        total = total + weight[(4, *here)] * pltpu.roll(centre, 127, 2)
        other = other + weight[(5, *here)] * pltpu.roll(centre, 1, 2)
        return total + other

    def first_sweep(level):
        index = level.index
        first, blk, times = level.span(level.reach)

        def step(i):
            here = (pl.ds(first + i * blk, blk), pl.ds(*level.wide), slice(None))
            one[index][here] = inv[index][here] * right[index][here]

        loop(times, step)

    def sweep(level, source, target, radius):
        first, blk, times = level.span(radius)
        y, cy = level.mid if radius else level.core

        def step(i):
            x = first + i * blk
            here = (pl.ds(x, blk), pl.ds(y, cy), slice(None))
            centre = source[here]
            target[here] = 0.2 * centre + pulled(level, source, x, blk, y, cy, centre)

        loop(times, step)

    def residual(level, radius, columns):
        index = level.index
        first, blk, times = level.span(radius)
        y, cy = columns

        def step(i):
            x = first + i * blk
            here = (pl.ds(x, blk), pl.ds(y, cy), slice(None))
            centre = two[index][here]
            total = pulled(level, two[index], x, blk, y, cy, centre)
            tri[index][here] = dia[index][here] * (total - 0.8 * centre)

        loop(times, step)

    def lift(value, level, x, y, count):
        for row in (x, x + 1):
            for column in (y, y + 1):
                spot = (row, pl.ds(column, count, stride=2), slice(None))
                two[level.index][spot] = two[level.index][spot] + value

    zero, one_, two_, three, four, five = levels

    barrier = pltpu.get_barrier_semaphore()
    greeted = around(zero, zero.reach + 1) + ([(0, 2), (0, -2)] if gy_count > 4 else [])
    for dx, dy in greeted:
        pl.semaphore_signal(barrier, inc=1, device_id=device(dx, dy), device_id_type=MESH)
    loads = []
    for position, (source, target) in enumerate(
        (
            (tis_ref, tis.at[zero.own_x, zero.own_y]),
            (src_ref, right[0].at[zero.own_x, zero.own_y]),
            (dif_ref, dif),
            (upt_ref, upt),
        )
    ):
        copy = pltpu.make_async_copy(source, target, local_sem.at[position])
        copy.start()
        loads.append(copy)
    pl.semaphore_wait(barrier, len(greeted))

    sent_tis = send_block(tis, zero, zero.reach + 1, (), 0, tis_ref)
    sent_src = send_block(right[0], zero, zero.reach, (), 0, src_ref)
    for level in (three, four, five):
        index = level.index
        for ref in (coef[index].at[0], one[index], two[index], tri[index]):
            ref[:, pl.ds(0, 8), :] = jnp.zeros((level.nx, 8, 128), F32)
            ref[:, pl.ds(8 + level.columns, 8), :] = jnp.zeros((level.nx, 8, 128), F32)
    for copy in loads:
        copy.wait()
    loop(zero.rows // 2, lambda i: types(zero.ox + 2 * i, 2, zero.oy, zero.columns))

    def coarsen(fine, level, known):
        for field in (0, 1):

            def step(i):
                value = mean(
                    coef[fine.index],
                    (field,),
                    fine.ox + 2 * (i - known),
                    fine.oy - 2 * known,
                    level.columns + 2 * known,
                )
                here = (level.ox - known + i, pl.ds(level.oy - known, level.columns + 2 * known), slice(None))
                coef[level.index][(field, *here)] = value

            loop(level.rows + 2 * known, step)

    coarsen(zero, one_, 0)
    both = (slice(None),)
    sent_c1 = send_block(coef[1], one_, one_.reach + 1, both)
    weights(zero, (zero.ox + 1, (zero.rows - 2) // 2, 2), zero.core, True)

    arrived(sent_tis)
    ring = zero.reach + 1
    types(zero.ox - ring, ring, 8, zero.mid[1])
    types(zero.ox + zero.rows, ring, 8, zero.mid[1])
    loop(zero.rows // 8, lambda i: types(zero.ox + 8 * i, 8, 8, ring))
    loop(zero.rows // 8, lambda i: types(zero.ox + 8 * i, 8, zero.oy + zero.columns, ring))
    arrived(sent_src)
    weights(zero, (zero.ox - zero.reach, zero.reach + 1, 1), zero.wide, True)
    weights(zero, (zero.ox + zero.rows - 1, zero.reach + 1, 1), zero.wide, True)
    weights(zero, (zero.ox + 1, (zero.rows - 2) // 2, 2), (8, 8), True)
    weights(zero, (zero.ox + 1, (zero.rows - 2) // 2, 2), (zero.oy + zero.columns - 4, 8), True)

    def restrict_to(fine, level, known):
        def step(i):
            value = mean(tri[fine.index], (), fine.ox + 2 * (i - known), fine.oy - 2 * known, level.columns + 2 * known)
            right[level.index][level.ox - known + i, pl.ds(level.oy - known, level.columns + 2 * known), :] = value

        loop(level.rows + 2 * known, step)

    sweep(zero, one[0], two[0], zero.reach - 1)
    residual(zero, 0, zero.core)
    restrict_to(zero, one_, 0)
    sent_b1 = send_block(right[1], one_, one_.reach)
    left(sent_tis)
    left(sent_src)
    arrived(sent_c1)
    coarsen(one_, two_, 2)
    sent_c2 = send_block(coef[2], two_, two_.reach + 1, both, 2)
    weights(one_)
    left(sent_c1)

    arrived(sent_b1)
    first_sweep(one_)
    sweep(one_, one[1], two[1], one_.reach - 1)
    residual(one_, 2, one_.mid)
    restrict_to(one_, two_, 1)
    sent_b2 = send_block(right[2], two_, two_.reach, (), 1)
    arrived(sent_c2)
    for field in (0, 1):
        for row in range(4):
            gat_c[gy, field, row] = mean(coef[2], (field,), two_.ox - 2 + 2 * row, two_.oy, 4)
    sent_c3 = send_columns(gat_c)
    weights(two_)
    left(sent_c2)
    left(sent_b1)

    arrived(sent_b2)
    first_sweep(two_)
    sweep(two_, one[2], two[2], two_.reach - 1)
    residual(two_, 2, two_.core)
    for row in range(4):
        gat_b[gy, row] = mean(tri[2], (), two_.ox - 2 + 2 * row, two_.oy, 4)
    sent_b3 = send_columns(gat_b)

    def unpack(read, write):
        for part in range(gy_count):
            for row in range(4):
                write(row, pl.ds(8 + 4 * part, 4), read(part, row))

    arrived(sent_c3)
    for field in (0, 1):

        def write(row, columns, value):
            coef[3][field, three.ox - 1 + row, columns, :] = value

        unpack(lambda part, row: gat_c[part, field, row], write)
    moves = ((2, -1, -5, 4), (-2, -1, 3, 4))
    sent_x3 = send_known(coef[3], three, (*moves, (3, 0, -6, 1), (-3, 1, 7, 1)), 1, both)
    left(sent_b2)
    left(sent_c3)

    arrived(sent_b3)

    def write_right(row, columns, value):
        right[3][three.ox - 1 + row, columns, :] = value

    unpack(lambda part, row: gat_b[part, row], write_right)
    sent_r3 = send_known(right[3], three, moves)
    arrived(sent_x3)
    for row in range(-3, 4):
        for field in (0, 1):
            value = mean(coef[3], (field,), three.ox + 2 * row, 8, four.columns)
            coef[4][field, four.ox + row, four.own_y, :] = value
    sent_c4 = send_known(coef[4], four, ((3, -3, -6, 3), (-3, 1, 4, 3)), 1, both)
    weights(three)
    left(sent_x3)
    left(sent_b3)
    arrived(sent_r3)
    first_sweep(three)
    sweep(three, one[3], two[3], three.reach - 1)
    residual(three, 2, three.core)
    for row in (-1, 0, 1):
        right[4][four.ox + row, four.own_y, :] = mean(tri[3], (), three.ox + 2 * row, 8, four.columns)

    moves = ((4, -1, -5, 1), (-4, 1, 5, 1), (3, -1, -4, 3), (-3, -1, 2, 3))
    sent_r4 = send_known(right[4], four, moves)
    arrived(sent_c4)
    chip = four.ox - parity
    for row in range(-2, 3):
        for field in (0, 1):
            value = mean(coef[4], (field,), chip + 2 * row, 8, five.columns)
            coef[5][field, five.ox + row, five.own_y, :] = value
    sent_c5 = send_known(coef[5], five, ((4, -2, -6, 4), (-4, -1, 3, 4)), 2, both)
    weights(four)
    left(sent_r3)
    left(sent_c4)
    arrived(sent_r4)
    first_sweep(four)
    sweep(four, one[4], two[4], four.reach - 1)
    residual(four, 3, four.core)
    for row in (-1, 0, 1):
        right[5][five.ox + row, five.own_y, :] = mean(tri[4], (), chip + 2 * row, 8, five.columns)

    sent_r5 = send_known(right[5], five, moves, 2)
    arrived(sent_c5)
    weights(five)
    left(sent_r4)
    left(sent_c5)
    arrived(sent_r5)
    first_sweep(five)
    sweep(five, one[5], two[5], 4)
    sweep(five, two[5], tri[5], 3)
    sweep(five, tri[5], two[5], 2)
    left(sent_r5)

    def ascend(level, last):
        index = level.index
        sweep(level, two[index], tri[index], last + 1)
        sweep(level, tri[index], two[index], last)

    for offset in range(-4, 5):
        row = five.ox - 4 + (parity + (offset + 8)) // 2
        value = two[5][row, five.own_y, :]
        for column in (8, 9):
            spot = (four.ox + offset, pl.ds(column, five.columns, stride=2), slice(None))
            two[4][spot] = two[4][spot] + value
    ascend(four, 2)
    for offset in range(-2, 3):
        lift(two[4][four.ox + offset, four.own_y, :], three, three.ox + 2 * offset, 8, four.columns)
    ascend(three, 2)
    for offset in range(-2, 4):
        value = two[3][three.ox + offset, pl.ds(6 + 4 * gy, 8), :]
        lift(value, two_, two_.ox + 2 * offset, two_.oy - 4, 8)
    ascend(two_, 2)

    def lift_one(i):
        value = two[2][two_.ox - 2 + i, pl.ds(two_.oy - 2, two_.columns + 4), :]
        lift(value, one_, one_.ox - 4 + 2 * i, one_.oy - 4, two_.columns + 4)

    loop(two_.rows + 4, lift_one)
    ascend(one_, 1)

    def lift_zero(i):
        value = two[1][one_.ox - 1 + i, pl.ds(one_.oy - 1, one_.columns + 2), :]
        lift(value, zero, zero.ox - 2 + 2 * i, zero.oy - 2, one_.columns + 2)

    loop(one_.rows + 2, lift_zero)
    sweep(zero, two[0], tri[0], 1)
    y, cy = zero.core
    part = zero.rows // 4
    copies = []
    for chunk in range(4):
        x = zero.ox + chunk * part
        here = (pl.ds(x, part), pl.ds(y, cy), slice(None))
        centre = tri[0][here]
        two[0][here] = 0.2 * centre + pulled(zero, tri[0], x, part, y, cy, centre)
        copy = pltpu.make_async_copy(
            two[0].at[pl.ds(x, part), pl.ds(y, cy)], out_ref.at[pl.ds(chunk * part, part)], local_sem.at[chunk]
        )
        copy.start()
        copies.append(copy)
    for copy in copies:
        copy.wait()


def build(mesh, rows, columns):
    gx_count, gy_count = mesh.shape["gx"], mesh.shape["gy"]
    levels = [
        Level(0, rows, columns, False, 5),
        Level(1, rows // 2, columns // 2, False, 7),
        Level(2, rows // 4, columns // 4, False, 12),
        Level(3, rows // 8, columns // 8 * gy_count, True, 6),
        Level(4, rows // 16, columns // 16 * gy_count, True, 11),
        Level(5, 1, columns // 32 * gy_count, True, 11),
    ]
    zero = levels[0]
    messages = 96
    scratch = [pltpu.VMEM(zero.shape(), jnp.int32)]
    scratch += [pltpu.VMEM(level.shape(2), F32) for level in levels]
    scratch += [pltpu.VMEM(level.shape(), F32) for level in levels]
    scratch += [pltpu.VMEM(level.shape(6), F32) for level in levels]
    for _ in range(5):
        scratch += [pltpu.VMEM(level.shape(), F32) for level in levels]
    scratch += [
        pltpu.VMEM((gy_count, 2, 4, 4, 128), F32),
        pltpu.VMEM((gy_count, 4, 4, 128), F32),
        pltpu.SMEM((TYPES,), F32),
        pltpu.SMEM((TYPES,), F32),
        pltpu.SemaphoreType.DMA((4,)),
        pltpu.SemaphoreType.DMA((messages,)),
        pltpu.SemaphoreType.DMA((messages,)),
    ]
    return pl.pallas_call(
        functools.partial(kernel, (gx_count, gy_count), levels),
        out_shape=jax.ShapeDtypeStruct((rows, columns, 128), F32),
        in_specs=[
            pl.BlockSpec(memory_space=pltpu.HBM),
            pl.BlockSpec(memory_space=pltpu.HBM),
            pl.BlockSpec(memory_space=pltpu.HBM),
            pl.BlockSpec(memory_space=pltpu.HBM),
        ],
        out_specs=pl.BlockSpec(memory_space=pltpu.HBM),
        scratch_shapes=scratch,
        name="vcycle",
        compiler_params=pltpu.CompilerParams(
            collective_id=0, has_side_effects=True, vmem_limit_bytes=64 * 2**20
        ),
    )


def solution(mesh):
    def body(source, tissue, diffusivity, uptake):
        call = build(mesh, source.shape[0], source.shape[1])
        return call(source, tissue, diffusivity, uptake)

    in_specs = (P("gx", "gy", None), P("gx", "gy", None), P(), P())
    out_specs = P("gx", "gy", None)
    return jax.shard_map(body, mesh=mesh, in_specs=in_specs, out_specs=out_specs, check_vma=False)
```

```python
import functools

import jax
import jax.numpy as jnp
from jax import lax
from jax.experimental import pallas as pl
from jax.experimental.pallas import tpu as pltpu
from jax.sharding import PartitionSpec as P

MESH = pl.DeviceIdType.MESH
F32 = jnp.float32
LEVELS = 6
TYPES = 8
HZ = 0.5 * 0.015625
REACH = (3, 4, 5, 5, 5, 5)


class Level:
    def __init__(self, index, rows, columns, across, most):
        self.index, self.rows, self.columns, self.across, self.most = index, rows, columns, across, most
        self.reach = REACH[index]
        self.ox = self.reach + 1
        self.nx = rows + 2 * self.ox + 2
        if across:
            self.oy = 8
            self.wide = self.mid = self.core = (8, columns)
            self.ny = 8 + columns + 8
        else:
            self.oy = 12
            self.core = (12, columns)
            around = -(-(columns + 8) // 8) * 8
            self.mid = (8, around)
            self.wide = (8, around) if self.reach < 5 else (4, around + 8)
            self.ny = around + 16
        self.own_x = pl.ds(self.ox, rows)
        self.own_y = pl.ds(self.oy, columns)
        self.half = 0.5 * 0.25**index

    def shape(self, *lead):
        return (*lead, self.nx, self.ny, 128)

    def span(self, radius):
        count = self.rows + 2 * radius
        times = -(-count // self.most)
        return self.ox - radius, -(-count // times), times


def overlap(size, step, radius, known):
    if known:
        low, high = {1: (-radius, -known), 0: (-known, size + known), -1: (size + known, size + radius)}[step]
        return low + step * size, low, high - low
    low = max(-radius, -step * size)
    high = min(size + radius, (1 - step) * size)
    return low + step * size, low, high - low


def kernel(sizes, levels, src_ref, tis_ref, dif_ref, upt_ref, out_ref, *scratch):
    gx_count, gy_count = sizes
    names = iter(scratch)
    tis = next(names)
    coef = [next(names) for _ in levels]
    right = [next(names) for _ in levels]
    wgt = [next(names) for _ in levels]
    inv = [next(names) for _ in levels]
    dia = [next(names) for _ in levels]
    one = [next(names) for _ in levels]
    two = [next(names) for _ in levels]
    tri = [next(names) for _ in levels]
    gat_c, gat_b = next(names), next(names)
    dif, upt = next(names), next(names)
    local_sem, send_sem, recv_sem = next(names), next(names), next(names)

    gx = lax.axis_index("gx")
    gy = lax.axis_index("gy")
    parity = lax.rem(gx, 2)
    places = {}

    def device(dx, dy):
        if ("x", dx) not in places:
            places["x", dx] = lax.rem(gx + (dx + gx_count), gx_count) if dx else gx
        if ("y", dy) not in places:
            places["y", dy] = lax.rem(gy + (dy + gy_count), gy_count) if dy else gy
        return places["x", dx], places["y", dy]

    counter = [0]

    def remote(source, target, dx, dy):
        number = counter[0]
        counter[0] += 1
        copy = pltpu.make_async_remote_copy(
            src_ref=source,
            dst_ref=target,
            send_sem=send_sem.at[number],
            recv_sem=recv_sem.at[number],
            device_id=device(dx, dy),
            device_id_type=MESH,
        )
        copy.start()
        return copy

    def arrived(copies):
        for copy in copies:
            copy.wait_recv()

    def left(copies):
        for copy in copies:
            copy.wait_send()

    def around(level, radius, known=0):
        far = -(-(radius - known) // level.rows)
        return [(dx, dy) for dx in range(-far, far + 1) for dy in (-1, 0, 1) if (dx, dy) != (0, 0)]

    def send_block(ref, level, radius, lead=(), known=0, origin=None):
        copies = []
        for dx, dy in sorted(around(level, radius, known), key=lambda step: -abs(step[0]) - abs(step[1])):
            sx, tx, cx = overlap(level.rows, dx, radius, known)
            sy, ty, cy = overlap(level.columns, dy, radius, known)
            if origin is None:
                source = ref.at[(*lead, pl.ds(level.ox + sx, cx), pl.ds(level.oy + sy, cy))]
            else:
                source = origin.at[pl.ds(sx, cx), pl.ds(sy, cy)]
            target = ref.at[(*lead, pl.ds(level.ox + tx, cx), pl.ds(level.oy + ty, cy))]
            copies.append(remote(source, target, dx, dy))
        return copies

    def send_known(ref, level, moves, stride=1, lead=()):
        copies = []
        for step, sx, tx, cx in moves:
            source = ref.at[(*lead, pl.ds(level.ox + sx, cx), level.own_y)]
            target = ref.at[(*lead, pl.ds(level.ox + tx, cx), level.own_y)]
            copies.append(remote(source, target, step * stride, 0))
        return copies

    def send_columns(source, ref, level, moves, position, lead=()):
        columns = pl.ds(8 + 4 * gy, 4)
        target = ref.at[(*lead, pl.ds(level.ox - 1, 4), columns)]
        own = pltpu.make_async_copy(source, target, local_sem.at[position])
        own.start()
        copies = []
        for dy in sorted(range(gy_count), key=lambda step: -min(step, gy_count - step)):
            for dx, tx in moves:
                if dx or dy:
                    target = ref.at[(*lead, pl.ds(level.ox + tx, 4), columns)]
                    copies.append(remote(source, target, dx, dy))
        return own, copies

    def loop(count, step, unrolled=False):
        if unrolled:
            for i in range(count):
                step(i)
            return

        def body(i, carry):
            step(i)
            return carry

        lax.fori_loop(0, count, body, 0)

    def seam(level, shape, axis, start, last):
        if axis == 0:
            half = level.index == LEVELS - 1
            total = level.rows * (gx_count // 2 if half else gx_count)
            base = (gx // 2 if half else gx) * level.rows + start - level.ox
        else:
            total = level.columns * gy_count
            base = gy * level.columns + start - level.oy
        place = lax.broadcasted_iota(jnp.int32, shape, axis) + base
        if last:
            return (place == total - 1) | (place == -1)
        return (place == 0) | (place == total)

    def types(x, blk, y, cy):
        kind = tis[pl.ds(x, blk), pl.ds(y, cy), :]
        kappa = jnp.full(kind.shape, dif[0], F32)
        sigma = jnp.full(kind.shape, upt[0], F32)
        for index in range(1, TYPES):
            hit = kind == index
            kappa = jnp.where(hit, dif[index], kappa)
            sigma = jnp.where(hit, upt[index], sigma)
        coef[0][0, pl.ds(x, blk), pl.ds(y, cy), :] = kappa
        coef[0][1, pl.ds(x, blk), pl.ds(y, cy), :] = sigma

    def mean(ref, lead, x, y, count):
        even = pl.ds(y, count, stride=2)
        odd = pl.ds(y + 1, count, stride=2)
        near = ref[(*lead, x, even, slice(None))] + ref[(*lead, x + 1, even, slice(None))]
        far = ref[(*lead, x, odd, slice(None))] + ref[(*lead, x + 1, odd, slice(None))]
        return 0.25 * (near + far)

    def weights(level, rows=None, columns=None, start=False):
        index = level.index
        first, blk, times = rows or level.span(level.reach)
        y, cy = columns or level.wide
        half = level.half

        def step(i):
            x = first + i * blk
            here = (pl.ds(x, blk), pl.ds(y, cy), slice(None))
            field = coef[index].at[0]
            centre = field[here]
            plane = lax.broadcasted_iota(jnp.int32, centre.shape, 2)
            row, column = pl.ds(x, blk), pl.ds(y, cy)
            faces = [
                (half, field[pl.ds(x + 1, blk), column, :], seam(level, centre.shape, 0, x, True)),
                (half, field[pl.ds(x - 1, blk), column, :], seam(level, centre.shape, 0, x, False)),
            ]
            if level.across:
                faces += [
                    (half, field[row, pl.ds(y + 1, cy), :], None),
                    (half, field[row, pl.ds(y - 1, cy), :], None),
                ]
            else:
                faces += [
                    (half, field[row, pl.ds(y + 1, cy), :], seam(level, centre.shape, 1, y, True)),
                    (half, field[row, pl.ds(y - 1, cy), :], seam(level, centre.shape, 1, y, False)),
                ]
            faces += [
                (HZ, pltpu.roll(centre, 127, 2), plane == 127),
                (HZ, pltpu.roll(centre, 1, 2), plane == 0),
            ]
            diag = coef[index][(1, *here)]
            weight = []
            for scale, beyond, closed in faces:
                if closed is not None:
                    beyond = jnp.where(closed, 0.0, beyond)
                face = scale * (centre + beyond)
                diag = diag + face
                weight.append(face)
            inverse = 0.8 / diag
            dia[index][here] = 1.25 * diag
            if start:
                one[index][here] = inverse * right[index][here]
            else:
                inv[index][here] = inverse
            for number, (scale, beyond, closed) in enumerate(faces):
                value = inverse * weight[number]
                if closed is not None:
                    value = jnp.where(closed, 0.0, value)
                wgt[index][(number, *here)] = value

        loop(times, step, times < 3)

    def pulled(level, field, x, blk, y, cy, centre):
        index = level.index
        here = (pl.ds(x, blk), pl.ds(y, cy), slice(None))
        weight = wgt[index]
        total = one[index][here] + weight[(0, *here)] * field[pl.ds(x + 1, blk), pl.ds(y, cy), :]
        other = weight[(1, *here)] * field[pl.ds(x - 1, blk), pl.ds(y, cy), :]
        total = total + weight[(2, *here)] * field[pl.ds(x, blk), pl.ds(y + 1, cy), :]
        other = other + weight[(3, *here)] * field[pl.ds(x, blk), pl.ds(y - 1, cy), :]
        total = total + weight[(4, *here)] * pltpu.roll(centre, 127, 2)
        other = other + weight[(5, *here)] * pltpu.roll(centre, 1, 2)
        return total + other

    def first_sweep(level):
        index = level.index
        first, blk, times = level.span(level.reach)

        def step(i):
            here = (pl.ds(first + i * blk, blk), pl.ds(*level.wide), slice(None))
            one[index][here] = inv[index][here] * right[index][here]

        loop(times, step, True)

    def sweep(level, source, target, radius):
        first, blk, times = level.span(radius)
        y, cy = level.mid if radius else level.core

        def step(i):
            x = first + i * blk
            here = (pl.ds(x, blk), pl.ds(y, cy), slice(None))
            centre = source[here]
            target[here] = 0.2 * centre + pulled(level, source, x, blk, y, cy, centre)

        loop(times, step, True)

    def residual(level, radius, columns):
        index = level.index
        first, blk, times = level.span(radius)
        y, cy = columns

        def step(i):
            x = first + i * blk
            here = (pl.ds(x, blk), pl.ds(y, cy), slice(None))
            centre = two[index][here]
            total = pulled(level, two[index], x, blk, y, cy, centre)
            tri[index][here] = dia[index][here] * (total - 0.8 * centre)

        loop(times, step, True)

    def lift(value, level, x, y, count):
        for row in (x, x + 1):
            for column in (y, y + 1):
                spot = (row, pl.ds(column, count, stride=2), slice(None))
                two[level.index][spot] = two[level.index][spot] + value

    zero, one_, two_, three, four, five = levels

    barrier = pltpu.get_barrier_semaphore()
    greeted = around(zero, zero.reach + 1) + ([(0, 2), (0, -2)] if gy_count > 4 else [])
    for dx, dy in greeted:
        pl.semaphore_signal(barrier, inc=1, device_id=device(dx, dy), device_id_type=MESH)
    loads = []
    for position, (source, target) in enumerate(
        (
            (tis_ref, tis.at[zero.own_x, zero.own_y]),
            (src_ref, right[0].at[zero.own_x, zero.own_y]),
            (dif_ref, dif),
            (upt_ref, upt),
        )
    ):
        copy = pltpu.make_async_copy(source, target, local_sem.at[position])
        copy.start()
        loads.append(copy)
    pl.semaphore_wait(barrier, len(greeted))

    sent_tis = send_block(tis, zero, zero.reach + 1, (), 0, tis_ref)
    sent_src = send_block(right[0], zero, zero.reach, (), 0, src_ref)
    for level in (three, four, five):
        index = level.index
        for ref in (coef[index].at[0], one[index], two[index], tri[index]):
            ref[:, pl.ds(0, 8), :] = jnp.zeros((level.nx, 8, 128), F32)
            ref[:, pl.ds(8 + level.columns, 8), :] = jnp.zeros((level.nx, 8, 128), F32)
    for copy in loads:
        copy.wait()
    loop(zero.rows // 2, lambda i: types(zero.ox + 2 * i, 2, zero.oy, zero.columns))

    def coarsen(fine, level, known):
        for field in (0, 1):

            def step(i):
                value = mean(
                    coef[fine.index],
                    (field,),
                    fine.ox + 2 * (i - known),
                    fine.oy - 2 * known,
                    level.columns + 2 * known,
                )
                here = (level.ox - known + i, pl.ds(level.oy - known, level.columns + 2 * known), slice(None))
                coef[level.index][(field, *here)] = value

            loop(level.rows + 2 * known, step)

    coarsen(zero, one_, 0)
    both = (slice(None),)
    sent_c1 = send_block(coef[1], one_, one_.reach + 1, both)
    weights(zero, (zero.ox + 1, (zero.rows - 2) // 2, 2), zero.core, True)

    arrived(sent_tis)
    ring = zero.reach + 1
    types(zero.ox - ring, ring, 8, zero.mid[1])
    types(zero.ox + zero.rows, ring, 8, zero.mid[1])
    types(zero.ox, zero.rows, 8, ring)
    types(zero.ox, zero.rows, zero.oy + zero.columns, ring)
    arrived(sent_src)
    weights(zero, (zero.ox - zero.reach, zero.reach + 1, 1), zero.wide, True)
    weights(zero, (zero.ox + zero.rows - 1, zero.reach + 1, 1), zero.wide, True)
    weights(zero, (zero.ox + 1, zero.rows - 2, 1), (8, 8), True)
    weights(zero, (zero.ox + 1, zero.rows - 2, 1), (zero.oy + zero.columns - 4, 8), True)

    def restrict_to(fine, level, known):
        def step(i):
            value = mean(tri[fine.index], (), fine.ox + 2 * (i - known), fine.oy - 2 * known, level.columns + 2 * known)
            right[level.index][level.ox - known + i, pl.ds(level.oy - known, level.columns + 2 * known), :] = value

        loop(level.rows + 2 * known, step, True)

    sweep(zero, one[0], two[0], zero.reach - 1)
    residual(zero, 0, zero.core)
    restrict_to(zero, one_, 0)
    sent_b1 = send_block(right[1], one_, one_.reach)
    left(sent_tis)
    left(sent_src)
    arrived(sent_c1)
    coarsen(one_, two_, 2)
    sent_c2 = send_block(coef[2], two_, two_.reach + 1, both, 2)
    weights(one_)
    left(sent_c1)

    arrived(sent_b1)
    first_sweep(one_)
    sweep(one_, one[1], two[1], one_.reach - 1)
    residual(one_, 2, one_.mid)
    restrict_to(one_, two_, 1)
    sent_b2 = send_block(right[2], two_, two_.reach, (), 1)
    arrived(sent_c2)
    for field in (0, 1):
        for row in range(4):
            gat_c[field, row] = mean(coef[2], (field,), two_.ox - 2 + 2 * row, two_.oy, 4)
    own_c3, sent_c3 = send_columns(gat_c, coef[3], three, ((0, -1),), 0, both)
    weights(two_)
    left(sent_c2)
    left(sent_b1)

    arrived(sent_b2)
    first_sweep(two_)
    sweep(two_, one[2], two[2], two_.reach - 1)
    residual(two_, 2, two_.core)
    for row in range(4):
        gat_b[row] = mean(tri[2], (), two_.ox - 2 + 2 * row, two_.oy, 4)

    own_b3, sent_b3 = send_columns(gat_b, right[3], three, ((2, -5), (-2, 3), (0, -1)), 1)
    own_c3.wait()
    arrived(sent_c3)
    sent_x3 = send_known(coef[3], three, ((2, -1, -5, 4), (-2, -1, 3, 4), (3, 0, -6, 1), (-3, 1, 7, 1)), 1, both)
    left(sent_b2)
    left(sent_c3)
    arrived(sent_x3)
    for row in range(-3, 4):
        for field in (0, 1):
            value = mean(coef[3], (field,), three.ox + 2 * row, 8, four.columns)
            coef[4][field, four.ox + row, four.own_y, :] = value
    sent_c4 = send_known(coef[4], four, ((3, -3, -6, 3), (-3, 1, 4, 3)), 1, both)
    weights(three)
    left(sent_x3)
    own_b3.wait()
    arrived(sent_b3)
    first_sweep(three)
    sweep(three, one[3], two[3], three.reach - 1)
    residual(three, 2, three.core)
    for row in (-1, 0, 1):
        right[4][four.ox + row, four.own_y, :] = mean(tri[3], (), three.ox + 2 * row, 8, four.columns)

    moves = ((4, -1, -5, 1), (-4, 1, 5, 1), (3, -1, -4, 3), (-3, -1, 2, 3))
    sent_r4 = send_known(right[4], four, moves)
    arrived(sent_c4)
    chip = four.ox - parity
    for row in range(-2, 3):
        for field in (0, 1):
            value = mean(coef[4], (field,), chip + 2 * row, 8, five.columns)
            coef[5][field, five.ox + row, five.own_y, :] = value
    sent_c5 = send_known(coef[5], five, ((4, -2, -6, 4), (-4, -1, 3, 4)), 2, both)
    weights(four)
    left(sent_b3)
    left(sent_c4)
    arrived(sent_r4)
    first_sweep(four)
    sweep(four, one[4], two[4], four.reach - 1)
    residual(four, 3, four.core)
    for row in (-1, 0, 1):
        right[5][five.ox + row, five.own_y, :] = mean(tri[4], (), chip + 2 * row, 8, five.columns)

    sent_r5 = send_known(right[5], five, moves, 2)
    arrived(sent_c5)
    weights(five)
    left(sent_r4)
    left(sent_c5)
    arrived(sent_r5)
    first_sweep(five)
    sweep(five, one[5], two[5], 4)
    sweep(five, two[5], tri[5], 3)
    sweep(five, tri[5], two[5], 2)
    left(sent_r5)

    def ascend(level, last):
        index = level.index
        sweep(level, two[index], tri[index], last + 1)
        sweep(level, tri[index], two[index], last)

    for offset in range(-4, 5):
        row = five.ox - 4 + (parity + (offset + 8)) // 2
        value = two[5][row, five.own_y, :]
        for column in (8, 9):
            spot = (four.ox + offset, pl.ds(column, five.columns, stride=2), slice(None))
            two[4][spot] = two[4][spot] + value
    ascend(four, 2)
    for offset in range(-2, 3):
        lift(two[4][four.ox + offset, four.own_y, :], three, three.ox + 2 * offset, 8, four.columns)
    ascend(three, 2)
    for offset in range(-2, 4):
        value = two[3][three.ox + offset, pl.ds(6 + 4 * gy, 8), :]
        lift(value, two_, two_.ox + 2 * offset, two_.oy - 4, 8)
    ascend(two_, 2)

    def lift_one(i):
        value = two[2][two_.ox - 2 + i, pl.ds(two_.oy - 2, two_.columns + 4), :]
        lift(value, one_, one_.ox - 4 + 2 * i, one_.oy - 4, two_.columns + 4)

    loop(two_.rows + 4, lift_one, True)
    ascend(one_, 1)

    def lift_zero(i):
        value = two[1][one_.ox - 1 + i, pl.ds(one_.oy - 1, one_.columns + 2), :]
        lift(value, zero, zero.ox - 2 + 2 * i, zero.oy - 2, one_.columns + 2)

    loop(one_.rows + 2, lift_zero, True)
    sweep(zero, two[0], tri[0], 1)
    y, cy = zero.core
    part = zero.rows // 4
    copies = []
    for chunk in range(4):
        x = zero.ox + chunk * part
        for row in range(x, x + part, 2):
            here = (pl.ds(row, 2), pl.ds(y, cy), slice(None))
            centre = tri[0][here]
            two[0][here] = 0.2 * centre + pulled(zero, tri[0], row, 2, y, cy, centre)
        copy = pltpu.make_async_copy(
            two[0].at[pl.ds(x, part), pl.ds(y, cy)], out_ref.at[pl.ds(chunk * part, part)], local_sem.at[chunk]
        )
        copy.start()
        copies.append(copy)
    for copy in copies:
        copy.wait()


def build(mesh, rows, columns):
    gx_count, gy_count = mesh.shape["gx"], mesh.shape["gy"]
    levels = [
        Level(0, rows, columns, False, 2),
        Level(1, rows // 2, columns // 2, False, 3),
        Level(2, rows // 4, columns // 4, False, 12),
        Level(3, rows // 8, columns // 8 * gy_count, True, 4),
        Level(4, rows // 16, columns // 16 * gy_count, True, 11),
        Level(5, 1, columns // 32 * gy_count, True, 11),
    ]
    zero = levels[0]
    messages = 96
    scratch = [pltpu.VMEM(zero.shape(), jnp.int32)]
    scratch += [pltpu.VMEM(level.shape(2), F32) for level in levels]
    scratch += [pltpu.VMEM(level.shape(), F32) for level in levels]
    scratch += [pltpu.VMEM(level.shape(6), F32) for level in levels]
    for _ in range(5):
        scratch += [pltpu.VMEM(level.shape(), F32) for level in levels]
    scratch += [
        pltpu.VMEM((2, 4, 4, 128), F32),
        pltpu.VMEM((4, 4, 128), F32),
        pltpu.SMEM((TYPES,), F32),
        pltpu.SMEM((TYPES,), F32),
        pltpu.SemaphoreType.DMA((4,)),
        pltpu.SemaphoreType.DMA((messages,)),
        pltpu.SemaphoreType.DMA((messages,)),
    ]
    return pl.pallas_call(
        functools.partial(kernel, (gx_count, gy_count), levels),
        out_shape=jax.ShapeDtypeStruct((rows, columns, 128), F32),
        in_specs=[
            pl.BlockSpec(memory_space=pltpu.HBM),
            pl.BlockSpec(memory_space=pltpu.HBM),
            pl.BlockSpec(memory_space=pltpu.HBM),
            pl.BlockSpec(memory_space=pltpu.HBM),
        ],
        out_specs=pl.BlockSpec(memory_space=pltpu.HBM),
        scratch_shapes=scratch,
        name="vcycle",
        compiler_params=pltpu.CompilerParams(
            collective_id=0, has_side_effects=True, vmem_limit_bytes=64 * 2**20
        ),
    )


def solution(mesh):
    def body(source, tissue, diffusivity, uptake):
        call = build(mesh, source.shape[0], source.shape[1])
        return call(source, tissue, diffusivity, uptake)

    in_specs = (P("gx", "gy", None), P("gx", "gy", None), P(), P())
    out_specs = P("gx", "gy", None)
    return jax.shard_map(body, mesh=mesh, in_specs=in_specs, out_specs=out_specs, check_vma=False)
```

```python
import functools

import jax
import jax.numpy as jnp
from jax import lax
from jax.experimental import pallas as pl
from jax.experimental.pallas import tpu as pltpu
from jax.sharding import PartitionSpec as P

MESH = pl.DeviceIdType.MESH
F32 = jnp.float32
LEVELS = 6
TYPES = 8
HZ = 0.5 * 0.015625
REACH = (3, 4, 5, 5, 5, 5)


class Level:
    def __init__(self, index, rows, columns, across, most):
        self.index, self.rows, self.columns, self.across, self.most = index, rows, columns, across, most
        self.reach = REACH[index]
        self.ox = self.reach + 1
        self.nx = rows + 2 * self.ox + 2
        if across:
            self.oy = 8
            self.wide = self.mid = self.core = (8, columns)
            self.ny = 8 + columns + 8
        else:
            self.oy = 12
            self.core = (12, columns)
            around = -(-(columns + 8) // 8) * 8
            self.mid = (8, around)
            self.wide = (8, around) if self.reach < 5 else (4, around + 8)
            self.ny = around + 16
        self.own_x = pl.ds(self.ox, rows)
        self.own_y = pl.ds(self.oy, columns)
        self.half = 0.5 * 0.25**index

    def shape(self, *lead):
        return (*lead, self.nx, self.ny, 128)

    def span(self, radius):
        count = self.rows + 2 * radius
        times = -(-count // self.most)
        return self.ox - radius, -(-count // times), times


def overlap(size, step, radius, known):
    if known:
        low, high = {1: (-radius, -known), 0: (-known, size + known), -1: (size + known, size + radius)}[step]
        return low + step * size, low, high - low
    low = max(-radius, -step * size)
    high = min(size + radius, (1 - step) * size)
    return low + step * size, low, high - low


def kernel(sizes, levels, src_ref, tis_ref, dif_ref, upt_ref, out_ref, *scratch):
    gx_count, gy_count = sizes
    names = iter(scratch)
    tis = next(names)
    coef = [next(names) for _ in levels]
    right = [next(names) for _ in levels]
    wgt = [next(names) for _ in levels]
    inv = [next(names) for _ in levels]
    dia = [next(names) for _ in levels]
    one = [next(names) for _ in levels]
    two = [next(names) for _ in levels]
    tri = [next(names) for _ in levels]
    gat_c, gat_b = next(names), next(names)
    dif, upt = next(names), next(names)
    local_sem, send_sem, recv_sem = next(names), next(names), next(names)

    gx = lax.axis_index("gx")
    gy = lax.axis_index("gy")
    parity = lax.rem(gx, 2)
    places = {}

    def device(dx, dy):
        if ("x", dx) not in places:
            places["x", dx] = lax.rem(gx + (dx + gx_count), gx_count) if dx else gx
        if ("y", dy) not in places:
            places["y", dy] = lax.rem(gy + (dy + gy_count), gy_count) if dy else gy
        return places["x", dx], places["y", dy]

    counter = [0]

    def remote(source, target, dx, dy):
        number = counter[0]
        counter[0] += 1
        copy = pltpu.make_async_remote_copy(
            src_ref=source,
            dst_ref=target,
            send_sem=send_sem.at[number],
            recv_sem=recv_sem.at[number],
            device_id=device(dx, dy),
            device_id_type=MESH,
        )
        copy.start()
        return copy

    def arrived(copies):
        for copy in copies:
            copy.wait_recv()

    def left(copies):
        for copy in copies:
            copy.wait_send()

    def around(level, radius, known=0):
        far = -(-(radius - known) // level.rows)
        return [(dx, dy) for dx in range(-far, far + 1) for dy in (-1, 0, 1) if (dx, dy) != (0, 0)]

    def send_block(ref, level, radius, lead=(), known=0, origin=None):
        copies = []
        for dx, dy in sorted(around(level, radius, known), key=lambda step: -abs(step[0]) - abs(step[1])):
            sx, tx, cx = overlap(level.rows, dx, radius, known)
            sy, ty, cy = overlap(level.columns, dy, radius, known)
            if origin is None:
                source = ref.at[(*lead, pl.ds(level.ox + sx, cx), pl.ds(level.oy + sy, cy))]
            else:
                source = origin.at[pl.ds(sx, cx), pl.ds(sy, cy)]
            target = ref.at[(*lead, pl.ds(level.ox + tx, cx), pl.ds(level.oy + ty, cy))]
            copies.append(remote(source, target, dx, dy))
        return copies

    def send_known(ref, level, moves, stride=1, lead=()):
        copies = []
        for step, sx, tx, cx in moves:
            source = ref.at[(*lead, pl.ds(level.ox + sx, cx), level.own_y)]
            target = ref.at[(*lead, pl.ds(level.ox + tx, cx), level.own_y)]
            copies.append(remote(source, target, step * stride, 0))
        return copies

    def send_columns(source, ref, level, moves, position, lead=()):
        columns = pl.ds(8 + 4 * gy, 4)
        target = ref.at[(*lead, pl.ds(level.ox - 1, 4), columns)]
        own = pltpu.make_async_copy(source, target, local_sem.at[position])
        own.start()
        copies = []
        for dy in sorted(range(gy_count), key=lambda step: -min(step, gy_count - step)):
            for dx, tx in moves:
                if dx or dy:
                    target = ref.at[(*lead, pl.ds(level.ox + tx, 4), columns)]
                    copies.append(remote(source, target, dx, dy))
        return own, copies

    def loop(count, step, unrolled=False):
        if unrolled:
            for i in range(count):
                step(i)
            return

        def body(i, carry):
            step(i)
            return carry

        lax.fori_loop(0, count, body, 0)

    def seam(level, shape, axis, start, last):
        if axis == 0:
            half = level.index == LEVELS - 1
            total = level.rows * (gx_count // 2 if half else gx_count)
            base = (gx // 2 if half else gx) * level.rows + start - level.ox
        else:
            total = level.columns * gy_count
            base = gy * level.columns + start - level.oy
        place = lax.broadcasted_iota(jnp.int32, shape, axis) + base
        if last:
            return (place == total - 1) | (place == -1)
        return (place == 0) | (place == total)

    def types(x, blk, y, cy):
        kind = tis[pl.ds(x, blk), pl.ds(y, cy), :]
        kappa = jnp.full(kind.shape, dif[0], F32)
        sigma = jnp.full(kind.shape, upt[0], F32)
        for index in range(1, TYPES):
            hit = kind == index
            kappa = jnp.where(hit, dif[index], kappa)
            sigma = jnp.where(hit, upt[index], sigma)
        coef[0][0, pl.ds(x, blk), pl.ds(y, cy), :] = kappa
        coef[0][1, pl.ds(x, blk), pl.ds(y, cy), :] = sigma

    def mean(ref, lead, x, y, count):
        even = pl.ds(y, count, stride=2)
        odd = pl.ds(y + 1, count, stride=2)
        near = ref[(*lead, x, even, slice(None))] + ref[(*lead, x + 1, even, slice(None))]
        far = ref[(*lead, x, odd, slice(None))] + ref[(*lead, x + 1, odd, slice(None))]
        return 0.25 * (near + far)

    def weights(level, rows=None, columns=None, start=False):
        index = level.index
        first, blk, times = rows or level.span(level.reach)
        y, cy = columns or level.wide
        half = level.half

        def step(i):
            x = first + i * blk
            here = (pl.ds(x, blk), pl.ds(y, cy), slice(None))
            field = coef[index].at[0]
            centre = field[here]
            plane = lax.broadcasted_iota(jnp.int32, centre.shape, 2)
            row, column = pl.ds(x, blk), pl.ds(y, cy)
            faces = [
                (half, field[pl.ds(x + 1, blk), column, :], seam(level, centre.shape, 0, x, True)),
                (half, field[pl.ds(x - 1, blk), column, :], seam(level, centre.shape, 0, x, False)),
            ]
            if level.across:
                faces += [
                    (half, field[row, pl.ds(y + 1, cy), :], None),
                    (half, field[row, pl.ds(y - 1, cy), :], None),
                ]
            else:
                faces += [
                    (half, field[row, pl.ds(y + 1, cy), :], seam(level, centre.shape, 1, y, True)),
                    (half, field[row, pl.ds(y - 1, cy), :], seam(level, centre.shape, 1, y, False)),
                ]
            faces += [
                (HZ, pltpu.roll(centre, 127, 2), plane == 127),
                (HZ, pltpu.roll(centre, 1, 2), plane == 0),
            ]
            diag = coef[index][(1, *here)]
            weight = []
            for scale, beyond, closed in faces:
                if closed is not None:
                    beyond = jnp.where(closed, 0.0, beyond)
                face = scale * (centre + beyond)
                diag = diag + face
                weight.append(face)
            inverse = 0.8 / diag
            dia[index][here] = 1.25 * diag
            if start:
                one[index][here] = inverse * right[index][here]
            else:
                inv[index][here] = inverse
            for number, (scale, beyond, closed) in enumerate(faces):
                value = inverse * weight[number]
                if closed is not None:
                    value = jnp.where(closed, 0.0, value)
                wgt[index][(number, *here)] = value

        loop(times, step, times < 3)

    def pulled(level, field, x, blk, y, cy, centre):
        index = level.index
        here = (pl.ds(x, blk), pl.ds(y, cy), slice(None))
        weight = wgt[index]
        total = one[index][here] + weight[(0, *here)] * field[pl.ds(x + 1, blk), pl.ds(y, cy), :]
        other = weight[(1, *here)] * field[pl.ds(x - 1, blk), pl.ds(y, cy), :]
        total = total + weight[(2, *here)] * field[pl.ds(x, blk), pl.ds(y + 1, cy), :]
        other = other + weight[(3, *here)] * field[pl.ds(x, blk), pl.ds(y - 1, cy), :]
        total = total + weight[(4, *here)] * pltpu.roll(centre, 127, 2)
        other = other + weight[(5, *here)] * pltpu.roll(centre, 1, 2)
        return total + other

    def first_sweep(level):
        index = level.index
        first, blk, times = level.span(level.reach)

        def step(i):
            here = (pl.ds(first + i * blk, blk), pl.ds(*level.wide), slice(None))
            one[index][here] = inv[index][here] * right[index][here]

        loop(times, step, True)

    def sweep(level, source, target, radius):
        first, blk, times = level.span(radius)
        y, cy = level.mid if radius else level.core

        def step(i):
            x = first + i * blk
            here = (pl.ds(x, blk), pl.ds(y, cy), slice(None))
            centre = source[here]
            target[here] = 0.2 * centre + pulled(level, source, x, blk, y, cy, centre)

        loop(times, step, True)

    def residual(level, radius, columns):
        index = level.index
        first, blk, times = level.span(radius)
        y, cy = columns

        def step(i):
            x = first + i * blk
            here = (pl.ds(x, blk), pl.ds(y, cy), slice(None))
            centre = two[index][here]
            total = pulled(level, two[index], x, blk, y, cy, centre)
            tri[index][here] = dia[index][here] * (total - 0.8 * centre)

        loop(times, step, True)

    def lift(value, level, x, y, count):
        for row in (x, x + 1):
            for column in (y, y + 1):
                spot = (row, pl.ds(column, count, stride=2), slice(None))
                two[level.index][spot] = two[level.index][spot] + value

    zero, one_, two_, three, four, five = levels

    barrier = pltpu.get_barrier_semaphore()
    greeted = around(two_, two_.reach + 1) + ([(0, 2), (0, -2), (0, 3), (0, -3)] if gy_count > 6 else [])
    for dx, dy in greeted:
        pl.semaphore_signal(barrier, inc=1, device_id=device(dx, dy), device_id_type=MESH)
    loads = []
    for position, (source, target) in enumerate(
        (
            (tis_ref, tis.at[zero.own_x, zero.own_y]),
            (src_ref, right[0].at[zero.own_x, zero.own_y]),
            (dif_ref, dif),
            (upt_ref, upt),
        )
    ):
        copy = pltpu.make_async_copy(source, target, local_sem.at[position])
        copy.start()
        loads.append(copy)
    pl.semaphore_wait(barrier, len(greeted))

    sent_tis = send_block(tis, zero, zero.reach + 1, (), 0, tis_ref)
    sent_src = send_block(right[0], zero, zero.reach, (), 0, src_ref)
    for level in (three, four, five):
        index = level.index
        for ref in (coef[index].at[0], one[index], two[index], tri[index]):
            ref[:, pl.ds(0, 8), :] = jnp.zeros((level.nx, 8, 128), F32)
            ref[:, pl.ds(8 + level.columns, 8), :] = jnp.zeros((level.nx, 8, 128), F32)
    for copy in loads:
        copy.wait()
    loop(zero.rows // 2, lambda i: types(zero.ox + 2 * i, 2, zero.oy, zero.columns))

    def coarsen(fine, level, known):
        for field in (0, 1):

            def step(i):
                value = mean(
                    coef[fine.index],
                    (field,),
                    fine.ox + 2 * (i - known),
                    fine.oy - 2 * known,
                    level.columns + 2 * known,
                )
                here = (level.ox - known + i, pl.ds(level.oy - known, level.columns + 2 * known), slice(None))
                coef[level.index][(field, *here)] = value

            loop(level.rows + 2 * known, step)

    coarsen(zero, one_, 0)
    both = (slice(None),)
    sent_c1 = send_block(coef[1], one_, one_.reach + 1, both)
    coarsen(one_, two_, 0)
    sent_c2 = send_block(coef[2], two_, two_.reach + 1, both)
    weights(zero, (zero.ox + 1, (zero.rows - 2) // 2, 2), zero.core, True)

    arrived(sent_tis)
    ring = zero.reach + 1
    types(zero.ox - ring, ring, 8, zero.mid[1])
    types(zero.ox + zero.rows, ring, 8, zero.mid[1])
    types(zero.ox, zero.rows, 8, ring)
    types(zero.ox, zero.rows, zero.oy + zero.columns, ring)
    arrived(sent_src)
    weights(zero, (zero.ox - zero.reach, zero.reach + 1, 1), zero.wide, True)
    weights(zero, (zero.ox + zero.rows - 1, zero.reach + 1, 1), zero.wide, True)
    weights(zero, (zero.ox + 1, zero.rows - 2, 1), (8, 8), True)
    weights(zero, (zero.ox + 1, zero.rows - 2, 1), (zero.oy + zero.columns - 4, 8), True)

    def restrict_to(fine, level, known):
        def step(i):
            value = mean(tri[fine.index], (), fine.ox + 2 * (i - known), fine.oy - 2 * known, level.columns + 2 * known)
            right[level.index][level.ox - known + i, pl.ds(level.oy - known, level.columns + 2 * known), :] = value

        loop(level.rows + 2 * known, step, True)

    sweep(zero, one[0], two[0], zero.reach - 1)
    residual(zero, 0, zero.core)
    restrict_to(zero, one_, 0)
    sent_b1 = send_block(right[1], one_, one_.reach)
    left(sent_tis)
    left(sent_src)
    arrived(sent_c2)
    for field in (0, 1):
        for row in range(4):
            gat_c[field, row] = mean(coef[2], (field,), two_.ox - 2 + 2 * row, two_.oy, 4)
    own_c3, sent_c3 = send_columns(gat_c, coef[3], three, ((0, -1),), 0, both)
    arrived(sent_c1)
    weights(one_)
    left(sent_c1)
    left(sent_c2)

    arrived(sent_b1)
    first_sweep(one_)
    sweep(one_, one[1], two[1], one_.reach - 1)
    residual(one_, 2, one_.mid)
    restrict_to(one_, two_, 1)
    sent_b2 = send_block(right[2], two_, two_.reach, (), 1)
    own_c3.wait()
    arrived(sent_c3)
    sent_x3 = send_known(coef[3], three, ((2, -1, -5, 4), (-2, -1, 3, 4), (3, 0, -6, 1), (-3, 1, 7, 1)), 1, both)
    weights(two_)
    left(sent_c3)
    left(sent_b1)

    arrived(sent_b2)
    first_sweep(two_)
    sweep(two_, one[2], two[2], two_.reach - 1)
    residual(two_, 2, two_.core)
    for row in range(4):
        gat_b[row] = mean(tri[2], (), two_.ox - 2 + 2 * row, two_.oy, 4)

    own_b3, sent_b3 = send_columns(gat_b, right[3], three, ((2, -5), (-2, 3), (0, -1)), 1)
    left(sent_b2)
    arrived(sent_x3)
    for row in range(-3, 4):
        for field in (0, 1):
            value = mean(coef[3], (field,), three.ox + 2 * row, 8, four.columns)
            coef[4][field, four.ox + row, four.own_y, :] = value
    sent_c4 = send_known(coef[4], four, ((3, -3, -6, 3), (-3, 1, 4, 3)), 1, both)
    weights(three)
    left(sent_x3)
    own_b3.wait()
    arrived(sent_b3)
    first_sweep(three)
    sweep(three, one[3], two[3], three.reach - 1)
    residual(three, 2, three.core)
    for row in (-1, 0, 1):
        right[4][four.ox + row, four.own_y, :] = mean(tri[3], (), three.ox + 2 * row, 8, four.columns)

    moves = ((4, -1, -5, 1), (-4, 1, 5, 1), (3, -1, -4, 3), (-3, -1, 2, 3))
    sent_r4 = send_known(right[4], four, moves)
    arrived(sent_c4)
    chip = four.ox - parity
    for row in range(-2, 3):
        for field in (0, 1):
            value = mean(coef[4], (field,), chip + 2 * row, 8, five.columns)
            coef[5][field, five.ox + row, five.own_y, :] = value
    sent_c5 = send_known(coef[5], five, ((4, -2, -6, 4), (-4, -1, 3, 4)), 2, both)
    weights(four)
    left(sent_b3)
    left(sent_c4)
    arrived(sent_r4)
    first_sweep(four)
    sweep(four, one[4], two[4], four.reach - 1)
    residual(four, 3, four.core)
    for row in (-1, 0, 1):
        right[5][five.ox + row, five.own_y, :] = mean(tri[4], (), chip + 2 * row, 8, five.columns)

    sent_r5 = send_known(right[5], five, moves, 2)
    arrived(sent_c5)
    weights(five)
    left(sent_r4)
    left(sent_c5)
    arrived(sent_r5)
    first_sweep(five)
    sweep(five, one[5], two[5], 4)
    sweep(five, two[5], tri[5], 3)
    sweep(five, tri[5], two[5], 2)
    left(sent_r5)

    def ascend(level, last):
        index = level.index
        sweep(level, two[index], tri[index], last + 1)
        sweep(level, tri[index], two[index], last)

    for offset in range(-4, 5):
        row = five.ox - 4 + (parity + (offset + 8)) // 2
        value = two[5][row, five.own_y, :]
        for column in (8, 9):
            spot = (four.ox + offset, pl.ds(column, five.columns, stride=2), slice(None))
            two[4][spot] = two[4][spot] + value
    ascend(four, 2)
    for offset in range(-2, 3):
        lift(two[4][four.ox + offset, four.own_y, :], three, three.ox + 2 * offset, 8, four.columns)
    ascend(three, 2)
    for offset in range(-2, 4):
        value = two[3][three.ox + offset, pl.ds(6 + 4 * gy, 8), :]
        lift(value, two_, two_.ox + 2 * offset, two_.oy - 4, 8)
    ascend(two_, 2)

    def lift_one(i):
        value = two[2][two_.ox - 2 + i, pl.ds(two_.oy - 2, two_.columns + 4), :]
        lift(value, one_, one_.ox - 4 + 2 * i, one_.oy - 4, two_.columns + 4)

    loop(two_.rows + 4, lift_one, True)
    ascend(one_, 1)

    def lift_zero(i):
        value = two[1][one_.ox - 1 + i, pl.ds(one_.oy - 1, one_.columns + 2), :]
        lift(value, zero, zero.ox - 2 + 2 * i, zero.oy - 2, one_.columns + 2)

    loop(one_.rows + 2, lift_zero, True)
    sweep(zero, two[0], tri[0], 1)
    y, cy = zero.core
    part = zero.rows // 4
    copies = []
    for chunk in range(4):
        x = zero.ox + chunk * part
        for row in range(x, x + part, 2):
            here = (pl.ds(row, 2), pl.ds(y, cy), slice(None))
            centre = tri[0][here]
            two[0][here] = 0.2 * centre + pulled(zero, tri[0], row, 2, y, cy, centre)
        copy = pltpu.make_async_copy(
            two[0].at[pl.ds(x, part), pl.ds(y, cy)], out_ref.at[pl.ds(chunk * part, part)], local_sem.at[chunk]
        )
        copy.start()
        copies.append(copy)
    for copy in copies:
        copy.wait()


def build(mesh, rows, columns):
    gx_count, gy_count = mesh.shape["gx"], mesh.shape["gy"]
    levels = [
        Level(0, rows, columns, False, 2),
        Level(1, rows // 2, columns // 2, False, 3),
        Level(2, rows // 4, columns // 4, False, 12),
        Level(3, rows // 8, columns // 8 * gy_count, True, 4),
        Level(4, rows // 16, columns // 16 * gy_count, True, 11),
        Level(5, 1, columns // 32 * gy_count, True, 11),
    ]
    zero = levels[0]
    messages = 112
    scratch = [pltpu.VMEM(zero.shape(), jnp.int32)]
    scratch += [pltpu.VMEM(level.shape(2), F32) for level in levels]
    scratch += [pltpu.VMEM(level.shape(), F32) for level in levels]
    scratch += [pltpu.VMEM(level.shape(6), F32) for level in levels]
    for _ in range(5):
        scratch += [pltpu.VMEM(level.shape(), F32) for level in levels]
    scratch += [
        pltpu.VMEM((2, 4, 4, 128), F32),
        pltpu.VMEM((4, 4, 128), F32),
        pltpu.SMEM((TYPES,), F32),
        pltpu.SMEM((TYPES,), F32),
        pltpu.SemaphoreType.DMA((4,)),
        pltpu.SemaphoreType.DMA((messages,)),
        pltpu.SemaphoreType.DMA((messages,)),
    ]
    return pl.pallas_call(
        functools.partial(kernel, (gx_count, gy_count), levels),
        out_shape=jax.ShapeDtypeStruct((rows, columns, 128), F32),
        in_specs=[
            pl.BlockSpec(memory_space=pltpu.HBM),
            pl.BlockSpec(memory_space=pltpu.HBM),
            pl.BlockSpec(memory_space=pltpu.HBM),
            pl.BlockSpec(memory_space=pltpu.HBM),
        ],
        out_specs=pl.BlockSpec(memory_space=pltpu.HBM),
        scratch_shapes=scratch,
        name="vcycle",
        compiler_params=pltpu.CompilerParams(
            collective_id=0, has_side_effects=True, vmem_limit_bytes=64 * 2**20
        ),
    )


def solution(mesh):
    def body(source, tissue, diffusivity, uptake):
        call = build(mesh, source.shape[0], source.shape[1])
        return call(source, tissue, diffusivity, uptake)

    in_specs = (P("gx", "gy", None), P("gx", "gy", None), P(), P())
    out_specs = P("gx", "gy", None)
    return jax.shard_map(body, mesh=mesh, in_specs=in_specs, out_specs=out_specs, check_vma=False)
```

```python
import functools

import jax
import jax.numpy as jnp
from jax import lax
from jax.experimental import pallas as pl
from jax.experimental.pallas import tpu as pltpu
from jax.sharding import PartitionSpec as P

MESH = pl.DeviceIdType.MESH
F32 = jnp.float32
LEVELS = 6
TYPES = 8
HZ = 0.5 * 0.015625
REACH = (3, 4, 5, 5, 5, 5)


class Level:
    def __init__(self, index, rows, columns, across, most):
        self.index, self.rows, self.columns, self.across, self.most = index, rows, columns, across, most
        self.reach = REACH[index]
        self.ox = self.reach + 1
        self.nx = rows + 2 * self.ox + 2
        if across:
            self.oy = 8
            self.wide = self.mid = self.core = (8, columns)
            self.ny = 8 + columns + 8
        else:
            self.oy = 12
            self.core = (12, columns)
            around = -(-(columns + 8) // 8) * 8
            self.mid = (8, around)
            self.wide = (8, around) if self.reach < 5 else (4, around + 8)
            self.ny = around + 16
        self.own_x = pl.ds(self.ox, rows)
        self.own_y = pl.ds(self.oy, columns)
        self.half = 0.5 * 0.25**index

    def shape(self, *lead):
        return (*lead, self.nx, self.ny, 128)

    def span(self, radius):
        count = self.rows + 2 * radius
        times = -(-count // self.most)
        return self.ox - radius, -(-count // times), times


def overlap(size, step, radius, known):
    if known:
        low, high = {1: (-radius, -known), 0: (-known, size + known), -1: (size + known, size + radius)}[step]
        return low + step * size, low, high - low
    low = max(-radius, -step * size)
    high = min(size + radius, (1 - step) * size)
    return low + step * size, low, high - low


def kernel(sizes, levels, src_ref, tis_ref, types_ref, out_ref, *scratch):
    gx_count, gy_count = sizes
    names = iter(scratch)
    tis = next(names)
    coef = [next(names) for _ in levels]
    right = [next(names) for _ in levels]
    wgt = [next(names) for _ in levels]
    inv = [next(names) for _ in levels]
    dia = [next(names) for _ in levels]
    one = [next(names) for _ in levels]
    two = [next(names) for _ in levels]
    tri = [next(names) for _ in levels]
    gat_c, gat_b = next(names), next(names)
    table = next(names)
    local_sem, send_sem, recv_sem = next(names), next(names), next(names)

    gx = lax.axis_index("gx")
    gy = lax.axis_index("gy")
    parity = lax.rem(gx, 2)
    places = {}

    def device(dx, dy):
        if ("x", dx) not in places:
            places["x", dx] = lax.rem(gx + (dx + gx_count), gx_count) if dx else gx
        if ("y", dy) not in places:
            places["y", dy] = lax.rem(gy + (dy + gy_count), gy_count) if dy else gy
        return places["x", dx], places["y", dy]

    counter = [0]

    def remote(source, target, dx, dy):
        number = counter[0]
        counter[0] += 1
        copy = pltpu.make_async_remote_copy(
            src_ref=source,
            dst_ref=target,
            send_sem=send_sem.at[number],
            recv_sem=recv_sem.at[number],
            device_id=device(dx, dy),
            device_id_type=MESH,
        )
        copy.start()
        return copy

    def arrived(copies):
        for copy in copies:
            copy.wait_recv()

    def left(copies):
        for copy in copies:
            copy.wait_send()

    def around(level, radius, known=0):
        far = -(-(radius - known) // level.rows)
        return [(dx, dy) for dx in range(-far, far + 1) for dy in (-1, 0, 1) if (dx, dy) != (0, 0)]

    def send_block(ref, level, radius, lead=(), known=0, origin=None):
        copies = []
        for dx, dy in sorted(around(level, radius, known), key=lambda step: -abs(step[0]) - abs(step[1])):
            sx, tx, cx = overlap(level.rows, dx, radius, known)
            sy, ty, cy = overlap(level.columns, dy, radius, known)
            if origin is None:
                source = ref.at[(*lead, pl.ds(level.ox + sx, cx), pl.ds(level.oy + sy, cy))]
            else:
                source = origin.at[pl.ds(sx, cx), pl.ds(sy, cy)]
            target = ref.at[(*lead, pl.ds(level.ox + tx, cx), pl.ds(level.oy + ty, cy))]
            copies.append(remote(source, target, dx, dy))
        return copies

    def send_known(ref, level, moves, stride=1, lead=()):
        copies = []
        for step, sx, tx, cx in moves:
            source = ref.at[(*lead, pl.ds(level.ox + sx, cx), level.own_y)]
            target = ref.at[(*lead, pl.ds(level.ox + tx, cx), level.own_y)]
            copies.append(remote(source, target, step * stride, 0))
        return copies

    def send_columns(source, ref, level, moves, position, lead=()):
        columns = pl.ds(8 + 4 * gy, 4)
        target = ref.at[(*lead, pl.ds(level.ox - 1, 4), columns)]
        own = pltpu.make_async_copy(source, target, local_sem.at[position])
        own.start()
        copies = []
        for dy in sorted(range(gy_count), key=lambda step: -min(step, gy_count - step)):
            for dx, tx in moves:
                if dx or dy:
                    target = ref.at[(*lead, pl.ds(level.ox + tx, 4), columns)]
                    copies.append(remote(source, target, dx, dy))
        return own, copies

    def loop(count, step, unrolled=False):
        if unrolled:
            for i in range(count):
                step(i)
            return

        def body(i, carry):
            step(i)
            return carry

        lax.fori_loop(0, count, body, 0)

    def seam(level, shape, axis, start, last):
        if axis == 0:
            half = level.index == LEVELS - 1
            total = level.rows * (gx_count // 2 if half else gx_count)
            base = (gx // 2 if half else gx) * level.rows + start - level.ox
        else:
            total = level.columns * gy_count
            base = gy * level.columns + start - level.oy
        place = lax.broadcasted_iota(jnp.int32, shape, axis) + base
        if last:
            return (place == total - 1) | (place == -1)
        return (place == 0) | (place == total)

    def types(x, blk, y, cy):
        kind = tis[pl.ds(x, blk), pl.ds(y, cy), :]
        kappa = jnp.full(kind.shape, table[0], F32)
        sigma = jnp.full(kind.shape, table[TYPES], F32)
        for index in range(1, TYPES):
            hit = kind == index
            kappa = jnp.where(hit, table[index], kappa)
            sigma = jnp.where(hit, table[TYPES + index], sigma)
        coef[0][0, pl.ds(x, blk), pl.ds(y, cy), :] = kappa
        coef[0][1, pl.ds(x, blk), pl.ds(y, cy), :] = sigma

    def mean(ref, lead, x, y, count):
        even = pl.ds(y, count, stride=2)
        odd = pl.ds(y + 1, count, stride=2)
        near = ref[(*lead, x, even, slice(None))] + ref[(*lead, x + 1, even, slice(None))]
        far = ref[(*lead, x, odd, slice(None))] + ref[(*lead, x + 1, odd, slice(None))]
        return 0.25 * (near + far)

    def weights(level, rows=None, columns=None, start=False):
        index = level.index
        first, blk, times = rows or level.span(level.reach)
        y, cy = columns or level.wide
        half = level.half

        def step(i):
            x = first + i * blk
            here = (pl.ds(x, blk), pl.ds(y, cy), slice(None))
            field = coef[index].at[0]
            centre = field[here]
            plane = lax.broadcasted_iota(jnp.int32, centre.shape, 2)
            row, column = pl.ds(x, blk), pl.ds(y, cy)
            faces = [
                (half, field[pl.ds(x + 1, blk), column, :], seam(level, centre.shape, 0, x, True)),
                (half, field[pl.ds(x - 1, blk), column, :], seam(level, centre.shape, 0, x, False)),
            ]
            if level.across:
                faces += [
                    (half, field[row, pl.ds(y + 1, cy), :], None),
                    (half, field[row, pl.ds(y - 1, cy), :], None),
                ]
            else:
                faces += [
                    (half, field[row, pl.ds(y + 1, cy), :], seam(level, centre.shape, 1, y, True)),
                    (half, field[row, pl.ds(y - 1, cy), :], seam(level, centre.shape, 1, y, False)),
                ]
            faces += [
                (HZ, pltpu.roll(centre, 127, 2), plane == 127),
                (HZ, pltpu.roll(centre, 1, 2), plane == 0),
            ]
            diag = coef[index][(1, *here)]
            weight = []
            for scale, beyond, closed in faces:
                if closed is not None:
                    beyond = jnp.where(closed, 0.0, beyond)
                face = scale * (centre + beyond)
                diag = diag + face
                weight.append(face)
            inverse = 0.8 / diag
            dia[index][here] = 1.25 * diag
            if start:
                one[index][here] = inverse * right[index][here]
            else:
                inv[index][here] = inverse
            for number, (scale, beyond, closed) in enumerate(faces):
                value = inverse * weight[number]
                if closed is not None:
                    value = jnp.where(closed, 0.0, value)
                wgt[index][(number, *here)] = value

        loop(times, step, times < 3)

    def pulled(level, field, x, blk, y, cy, centre):
        index = level.index
        here = (pl.ds(x, blk), pl.ds(y, cy), slice(None))
        weight = wgt[index]
        total = one[index][here] + weight[(0, *here)] * field[pl.ds(x + 1, blk), pl.ds(y, cy), :]
        other = weight[(1, *here)] * field[pl.ds(x - 1, blk), pl.ds(y, cy), :]
        total = total + weight[(2, *here)] * field[pl.ds(x, blk), pl.ds(y + 1, cy), :]
        other = other + weight[(3, *here)] * field[pl.ds(x, blk), pl.ds(y - 1, cy), :]
        total = total + weight[(4, *here)] * pltpu.roll(centre, 127, 2)
        other = other + weight[(5, *here)] * pltpu.roll(centre, 1, 2)
        return total + other

    def first_sweep(level):
        index = level.index
        first, blk, times = level.span(level.reach)

        def step(i):
            here = (pl.ds(first + i * blk, blk), pl.ds(*level.wide), slice(None))
            one[index][here] = inv[index][here] * right[index][here]

        loop(times, step, True)

    def sweep(level, source, target, radius):
        first, blk, times = level.span(radius)
        y, cy = level.mid if radius else level.core

        def step(i):
            x = first + i * blk
            here = (pl.ds(x, blk), pl.ds(y, cy), slice(None))
            centre = source[here]
            target[here] = 0.2 * centre + pulled(level, source, x, blk, y, cy, centre)

        loop(times, step, True)

    def residual(level, radius, columns):
        index = level.index
        first, blk, times = level.span(radius)
        y, cy = columns

        def step(i):
            x = first + i * blk
            here = (pl.ds(x, blk), pl.ds(y, cy), slice(None))
            centre = two[index][here]
            total = pulled(level, two[index], x, blk, y, cy, centre)
            tri[index][here] = dia[index][here] * (total - 0.8 * centre)

        loop(times, step, True)

    def lift(value, level, x, y, count):
        for row in (x, x + 1):
            for column in (y, y + 1):
                spot = (row, pl.ds(column, count, stride=2), slice(None))
                two[level.index][spot] = two[level.index][spot] + value

    zero, one_, two_, three, four, five = levels

    barrier = pltpu.get_barrier_semaphore()
    greeted = around(two_, two_.reach + 1) + ([(0, 2), (0, -2), (0, 3), (0, -3)] if gy_count > 6 else [])
    for dx, dy in greeted:
        pl.semaphore_signal(barrier, inc=1, device_id=device(dx, dy), device_id_type=MESH)
    pl.semaphore_wait(barrier, len(greeted))

    sent_tis = send_block(tis, zero, zero.reach + 1, (), 0, tis_ref)
    sent_src = send_block(right[0], zero, zero.reach, (), 0, src_ref)
    loads = []
    for position, (source, target) in enumerate(
        (
            (tis_ref, tis.at[zero.own_x, zero.own_y]),
            (src_ref, right[0].at[zero.own_x, zero.own_y]),
            (types_ref, table),
        )
    ):
        copy = pltpu.make_async_copy(source, target, local_sem.at[position])
        copy.start()
        loads.append(copy)
    for level in (three, four, five):
        index = level.index
        for ref in (coef[index].at[0], one[index], two[index], tri[index]):
            ref[:, pl.ds(0, 8), :] = jnp.zeros((level.nx, 8, 128), F32)
            ref[:, pl.ds(8 + level.columns, 8), :] = jnp.zeros((level.nx, 8, 128), F32)
    for copy in loads:
        copy.wait()
    loop(zero.rows // 2, lambda i: types(zero.ox + 2 * i, 2, zero.oy, zero.columns))

    def coarsen(fine, level, known):
        for field in (0, 1):

            def step(i):
                value = mean(
                    coef[fine.index],
                    (field,),
                    fine.ox + 2 * (i - known),
                    fine.oy - 2 * known,
                    level.columns + 2 * known,
                )
                here = (level.ox - known + i, pl.ds(level.oy - known, level.columns + 2 * known), slice(None))
                coef[level.index][(field, *here)] = value

            loop(level.rows + 2 * known, step)

    coarsen(zero, one_, 0)
    both = (slice(None),)
    sent_c1 = send_block(coef[1], one_, one_.reach + 1, both)
    coarsen(one_, two_, 0)
    sent_c2 = send_block(coef[2], two_, two_.reach + 1, both)
    weights(zero, (zero.ox + 1, (zero.rows - 2) // 2, 2), zero.core, True)

    arrived(sent_tis)
    ring = zero.reach + 1
    types(zero.ox - ring, ring, 8, zero.mid[1])
    types(zero.ox + zero.rows, ring, 8, zero.mid[1])
    types(zero.ox, zero.rows, 8, ring)
    types(zero.ox, zero.rows, zero.oy + zero.columns, ring)
    arrived(sent_src)
    weights(zero, (zero.ox - zero.reach, zero.reach + 1, 1), zero.wide, True)
    weights(zero, (zero.ox + zero.rows - 1, zero.reach + 1, 1), zero.wide, True)
    weights(zero, (zero.ox + 1, zero.rows - 2, 1), (8, 8), True)
    weights(zero, (zero.ox + 1, zero.rows - 2, 1), (zero.oy + zero.columns - 4, 8), True)

    def restrict_to(fine, level, known):
        def step(i):
            value = mean(tri[fine.index], (), fine.ox + 2 * (i - known), fine.oy - 2 * known, level.columns + 2 * known)
            right[level.index][level.ox - known + i, pl.ds(level.oy - known, level.columns + 2 * known), :] = value

        loop(level.rows + 2 * known, step, True)

    sweep(zero, one[0], two[0], zero.reach - 1)
    residual(zero, 0, zero.core)
    restrict_to(zero, one_, 0)
    sent_b1 = send_block(right[1], one_, one_.reach)
    left(sent_tis)
    left(sent_src)
    arrived(sent_c2)
    for field in (0, 1):
        for row in range(4):
            gat_c[field, row] = mean(coef[2], (field,), two_.ox - 2 + 2 * row, two_.oy, 4)
    own_c3, sent_c3 = send_columns(gat_c, coef[3], three, ((0, -1),), 0, both)
    arrived(sent_c1)
    weights(one_)
    left(sent_c1)
    left(sent_c2)

    arrived(sent_b1)
    first_sweep(one_)
    sweep(one_, one[1], two[1], one_.reach - 1)
    residual(one_, 2, one_.mid)
    restrict_to(one_, two_, 1)
    sent_b2 = send_block(right[2], two_, two_.reach, (), 1)
    own_c3.wait()
    arrived(sent_c3)
    sent_x3 = send_known(coef[3], three, ((2, -1, -5, 4), (-2, -1, 3, 4), (3, 0, -6, 1), (-3, 1, 7, 1)), 1, both)
    weights(two_)
    left(sent_c3)
    left(sent_b1)

    arrived(sent_b2)
    first_sweep(two_)
    sweep(two_, one[2], two[2], two_.reach - 1)
    residual(two_, 2, two_.core)
    for row in range(4):
        gat_b[row] = mean(tri[2], (), two_.ox - 2 + 2 * row, two_.oy, 4)

    own_b3, sent_b3 = send_columns(gat_b, right[3], three, ((2, -5), (-2, 3), (0, -1)), 1)
    left(sent_b2)
    arrived(sent_x3)
    for row in range(-3, 4):
        for field in (0, 1):
            value = mean(coef[3], (field,), three.ox + 2 * row, 8, four.columns)
            coef[4][field, four.ox + row, four.own_y, :] = value
    sent_c4 = send_known(coef[4], four, ((3, -3, -6, 3), (-3, 1, 4, 3)), 1, both)
    weights(three)
    left(sent_x3)
    own_b3.wait()
    arrived(sent_b3)
    first_sweep(three)
    sweep(three, one[3], two[3], three.reach - 1)
    residual(three, 2, three.core)
    for row in (-1, 0, 1):
        right[4][four.ox + row, four.own_y, :] = mean(tri[3], (), three.ox + 2 * row, 8, four.columns)

    moves = ((4, -1, -5, 1), (-4, 1, 5, 1), (3, -1, -4, 3), (-3, -1, 2, 3))
    sent_r4 = send_known(right[4], four, moves)
    arrived(sent_c4)
    chip = four.ox - parity
    for row in range(-2, 3):
        for field in (0, 1):
            value = mean(coef[4], (field,), chip + 2 * row, 8, five.columns)
            coef[5][field, five.ox + row, five.own_y, :] = value
    sent_c5 = send_known(coef[5], five, ((4, -2, -6, 4), (-4, -1, 3, 4)), 2, both)
    weights(four)
    left(sent_b3)
    left(sent_c4)
    arrived(sent_r4)
    first_sweep(four)
    sweep(four, one[4], two[4], four.reach - 1)
    residual(four, 3, four.core)
    for row in (-1, 0, 1):
        right[5][five.ox + row, five.own_y, :] = mean(tri[4], (), chip + 2 * row, 8, five.columns)

    sent_r5 = send_known(right[5], five, moves, 2)
    arrived(sent_c5)
    weights(five)
    left(sent_r4)
    left(sent_c5)
    arrived(sent_r5)
    first_sweep(five)
    sweep(five, one[5], two[5], 4)
    sweep(five, two[5], tri[5], 3)
    sweep(five, tri[5], two[5], 2)
    left(sent_r5)

    def ascend(level, last):
        index = level.index
        sweep(level, two[index], tri[index], last + 1)
        sweep(level, tri[index], two[index], last)

    for offset in range(-4, 5):
        row = five.ox - 4 + (parity + (offset + 8)) // 2
        value = two[5][row, five.own_y, :]
        for column in (8, 9):
            spot = (four.ox + offset, pl.ds(column, five.columns, stride=2), slice(None))
            two[4][spot] = two[4][spot] + value
    ascend(four, 2)
    for offset in range(-2, 3):
        lift(two[4][four.ox + offset, four.own_y, :], three, three.ox + 2 * offset, 8, four.columns)
    ascend(three, 2)
    for offset in range(-2, 4):
        value = two[3][three.ox + offset, pl.ds(6 + 4 * gy, 8), :]
        lift(value, two_, two_.ox + 2 * offset, two_.oy - 4, 8)
    ascend(two_, 2)

    def lift_one(i):
        value = two[2][two_.ox - 2 + i, pl.ds(two_.oy - 2, two_.columns + 4), :]
        lift(value, one_, one_.ox - 4 + 2 * i, one_.oy - 4, two_.columns + 4)

    loop(two_.rows + 4, lift_one, True)
    ascend(one_, 1)

    def lift_zero(i):
        value = two[1][one_.ox - 1 + i, pl.ds(one_.oy - 1, one_.columns + 2), :]
        lift(value, zero, zero.ox - 2 + 2 * i, zero.oy - 2, one_.columns + 2)

    loop(one_.rows + 2, lift_zero, True)
    sweep(zero, two[0], tri[0], 1)
    y, cy = zero.core
    for row in range(0, zero.rows, 2):
        here = (pl.ds(zero.ox + row, 2), pl.ds(y, cy), slice(None))
        centre = tri[0][here]
        out_ref[pl.ds(row, 2)] = 0.2 * centre + pulled(zero, tri[0], zero.ox + row, 2, y, cy, centre)


def build(mesh, rows, columns):
    gx_count, gy_count = mesh.shape["gx"], mesh.shape["gy"]
    levels = [
        Level(0, rows, columns, False, 2),
        Level(1, rows // 2, columns // 2, False, 3),
        Level(2, rows // 4, columns // 4, False, 12),
        Level(3, rows // 8, columns // 8 * gy_count, True, 4),
        Level(4, rows // 16, columns // 16 * gy_count, True, 11),
        Level(5, 1, columns // 32 * gy_count, True, 11),
    ]
    zero = levels[0]
    messages = 112
    scratch = [pltpu.VMEM(zero.shape(), jnp.int32)]
    scratch += [pltpu.VMEM(level.shape(2), F32) for level in levels]
    scratch += [pltpu.VMEM(level.shape(), F32) for level in levels]
    scratch += [pltpu.VMEM(level.shape(6), F32) for level in levels]
    for _ in range(5):
        scratch += [pltpu.VMEM(level.shape(), F32) for level in levels]
    scratch += [
        pltpu.VMEM((2, 4, 4, 128), F32),
        pltpu.VMEM((4, 4, 128), F32),
        pltpu.SMEM((2 * TYPES,), F32),
        pltpu.SemaphoreType.DMA((4,)),
        pltpu.SemaphoreType.DMA((messages,)),
        pltpu.SemaphoreType.DMA((messages,)),
    ]
    return pl.pallas_call(
        functools.partial(kernel, (gx_count, gy_count), levels),
        out_shape=jax.ShapeDtypeStruct((rows, columns, 128), F32),
        in_specs=[
            pl.BlockSpec(memory_space=pltpu.HBM),
            pl.BlockSpec(memory_space=pltpu.HBM),
            pl.BlockSpec(memory_space=pltpu.HBM),
        ],
        out_specs=pl.BlockSpec(memory_space=pltpu.VMEM),
        scratch_shapes=scratch,
        name="vcycle",
        compiler_params=pltpu.CompilerParams(
            collective_id=0, has_side_effects=True, vmem_limit_bytes=56_250_000
        ),
    )


def solution(mesh):
    def body(source, tissue, diffusivity, uptake):
        call = build(mesh, source.shape[0], source.shape[1])
        return call(source, tissue, jnp.concatenate([diffusivity, uptake]))

    in_specs = (P("gx", "gy", None), P("gx", "gy", None), P(), P())
    out_specs = P("gx", "gy", None)
    return jax.shard_map(body, mesh=mesh, in_specs=in_specs, out_specs=out_specs, check_vma=False)
```

```python
import functools

import jax
import jax.numpy as jnp
from jax import lax
from jax.experimental import pallas as pl
from jax.experimental.pallas import tpu as pltpu
from jax.sharding import PartitionSpec as P

MESH = pl.DeviceIdType.MESH
F32 = jnp.float32
LEVELS = 6
TYPES = 8
HZ = 0.5 * 0.015625
REACH = (3, 4, 5, 5, 5, 5)


class Level:
    def __init__(self, index, rows, columns, across, most):
        self.index, self.rows, self.columns, self.across, self.most = index, rows, columns, across, most
        self.reach = REACH[index]
        self.ox = self.reach + 1
        self.nx = rows + 2 * self.ox + 2
        if across:
            self.oy = 8
            self.wide = self.mid = self.core = (8, columns)
            self.ny = 8 + columns + 8
        else:
            self.oy = 12
            self.core = (12, columns)
            around = -(-(columns + 8) // 8) * 8
            self.mid = (8, around)
            self.wide = (8, around) if self.reach < 5 else (4, around + 8)
            self.ny = around + 16
        self.own_x = pl.ds(self.ox, rows)
        self.own_y = pl.ds(self.oy, columns)
        self.half = 0.5 * 0.25**index

    def shape(self, *lead):
        return (*lead, self.nx, self.ny, 128)

    def span(self, radius):
        count = self.rows + 2 * radius
        times = -(-count // self.most)
        return self.ox - radius, -(-count // times), times


def overlap(size, step, radius, known):
    if known:
        low, high = {1: (-radius, -known), 0: (-known, size + known), -1: (size + known, size + radius)}[step]
        return low + step * size, low, high - low
    low = max(-radius, -step * size)
    high = min(size + radius, (1 - step) * size)
    return low + step * size, low, high - low


def kernel(sizes, levels, src_ref, tis_ref, types_ref, out_ref, *scratch):
    gx_count, gy_count = sizes
    names = iter(scratch)
    tis = next(names)
    coef = [next(names) for _ in levels]
    right = [next(names) for _ in levels]
    wgt = [next(names) for _ in levels]
    inv = [next(names) for _ in levels]
    dia = [next(names) for _ in levels]
    one = [next(names) for _ in levels]
    two = [next(names) for _ in levels]
    tri = [next(names) for _ in levels]
    gat_c, gat_b = next(names), next(names)
    table = next(names)
    local_sem, send_sem, recv_sem = next(names), next(names), next(names)

    gx = lax.axis_index("gx")
    gy = lax.axis_index("gy")
    parity = lax.rem(gx, 2)
    places = {}

    def device(dx, dy):
        if ("x", dx) not in places:
            places["x", dx] = lax.rem(gx + (dx + gx_count), gx_count) if dx else gx
        if ("y", dy) not in places:
            places["y", dy] = lax.rem(gy + (dy + gy_count), gy_count) if dy else gy
        return places["x", dx], places["y", dy]

    counter = [0]

    def remote(source, target, dx, dy):
        number = counter[0]
        counter[0] += 1
        copy = pltpu.make_async_remote_copy(
            src_ref=source,
            dst_ref=target,
            send_sem=send_sem.at[number],
            recv_sem=recv_sem.at[number],
            device_id=device(dx, dy),
            device_id_type=MESH,
        )
        copy.start()
        return copy

    def arrived(copies):
        for copy in copies:
            copy.wait_recv()

    def left(copies):
        for copy in copies:
            copy.wait_send()

    def around(level, radius, known=0):
        far = -(-(radius - known) // level.rows)
        return [(dx, dy) for dx in range(-far, far + 1) for dy in (-1, 0, 1) if (dx, dy) != (0, 0)]

    def send_block(ref, level, radius, lead=(), known=0, origin=None):
        copies = []
        for dx, dy in sorted(around(level, radius, known), key=lambda step: -abs(step[0]) - abs(step[1])):
            sx, tx, cx = overlap(level.rows, dx, radius, known)
            sy, ty, cy = overlap(level.columns, dy, radius, known)
            if origin is None:
                source = ref.at[(*lead, pl.ds(level.ox + sx, cx), pl.ds(level.oy + sy, cy))]
            else:
                source = origin.at[pl.ds(sx, cx), pl.ds(sy, cy)]
            target = ref.at[(*lead, pl.ds(level.ox + tx, cx), pl.ds(level.oy + ty, cy))]
            copies.append(remote(source, target, dx, dy))
        return copies

    def send_known(ref, level, moves, stride=1, lead=()):
        copies = []
        for step, sx, tx, cx in moves:
            source = ref.at[(*lead, pl.ds(level.ox + sx, cx), level.own_y)]
            target = ref.at[(*lead, pl.ds(level.ox + tx, cx), level.own_y)]
            copies.append(remote(source, target, step * stride, 0))
        return copies

    def send_columns(source, ref, level, moves, position, lead=()):
        columns = pl.ds(8 + 4 * gy, 4)
        target = ref.at[(*lead, pl.ds(level.ox - 1, 4), columns)]
        own = pltpu.make_async_copy(source, target, local_sem.at[position])
        own.start()
        copies = []
        for dy in sorted(range(gy_count), key=lambda step: -min(step, gy_count - step)):
            for dx, tx in moves:
                if dx or dy:
                    target = ref.at[(*lead, pl.ds(level.ox + tx, 4), columns)]
                    copies.append(remote(source, target, dx, dy))
        return own, copies

    def loop(count, step, unrolled=False):
        if unrolled:
            for i in range(count):
                step(i)
            return

        def body(i, carry):
            step(i)
            return carry

        lax.fori_loop(0, count, body, 0)

    def seam(level, shape, axis, start, last):
        if axis == 0:
            half = level.index == LEVELS - 1
            total = level.rows * (gx_count // 2 if half else gx_count)
            base = (gx // 2 if half else gx) * level.rows + start - level.ox
        else:
            total = level.columns * gy_count
            base = gy * level.columns + start - level.oy
        place = lax.broadcasted_iota(jnp.int32, shape, axis) + base
        if last:
            return (place == total - 1) | (place == -1)
        return (place == 0) | (place == total)

    def types(x, blk, y, cy):
        kind = tis[pl.ds(x, blk), pl.ds(y, cy), :]
        kappa = jnp.full(kind.shape, table[0], F32)
        sigma = jnp.full(kind.shape, table[TYPES], F32)
        for index in range(1, TYPES):
            hit = kind == index
            kappa = jnp.where(hit, table[index], kappa)
            sigma = jnp.where(hit, table[TYPES + index], sigma)
        coef[0][0, pl.ds(x, blk), pl.ds(y, cy), :] = kappa
        coef[0][1, pl.ds(x, blk), pl.ds(y, cy), :] = sigma

    def mean(ref, lead, x, y, count):
        even = pl.ds(y, count, stride=2)
        odd = pl.ds(y + 1, count, stride=2)
        near = ref[(*lead, x, even, slice(None))] + ref[(*lead, x + 1, even, slice(None))]
        far = ref[(*lead, x, odd, slice(None))] + ref[(*lead, x + 1, odd, slice(None))]
        return 0.25 * (near + far)

    def weights(level, rows=None, columns=None, start=False):
        index = level.index
        first, blk, times = rows or level.span(level.reach)
        y, cy = columns or level.wide
        half = level.half

        def step(i):
            x = first + i * blk
            here = (pl.ds(x, blk), pl.ds(y, cy), slice(None))
            field = coef[index].at[0]
            centre = field[here]
            plane = lax.broadcasted_iota(jnp.int32, centre.shape, 2)
            row, column = pl.ds(x, blk), pl.ds(y, cy)
            faces = [
                (half, field[pl.ds(x + 1, blk), column, :], seam(level, centre.shape, 0, x, True)),
                (half, field[pl.ds(x - 1, blk), column, :], seam(level, centre.shape, 0, x, False)),
            ]
            if level.across:
                faces += [
                    (half, field[row, pl.ds(y + 1, cy), :], None),
                    (half, field[row, pl.ds(y - 1, cy), :], None),
                ]
            else:
                faces += [
                    (half, field[row, pl.ds(y + 1, cy), :], seam(level, centre.shape, 1, y, True)),
                    (half, field[row, pl.ds(y - 1, cy), :], seam(level, centre.shape, 1, y, False)),
                ]
            faces += [
                (HZ, pltpu.roll(centre, 127, 2), plane == 127),
                (HZ, pltpu.roll(centre, 1, 2), plane == 0),
            ]
            diag = coef[index][(1, *here)]
            weight = []
            for scale, beyond, closed in faces:
                if closed is not None:
                    beyond = jnp.where(closed, 0.0, beyond)
                face = scale * (centre + beyond)
                diag = diag + face
                weight.append(face)
            inverse = 0.8 / diag
            dia[index][here] = 1.25 * diag
            if start:
                one[index][here] = inverse * right[index][here]
            else:
                inv[index][here] = inverse
            for number, (scale, beyond, closed) in enumerate(faces):
                value = inverse * weight[number]
                if closed is not None:
                    value = jnp.where(closed, 0.0, value)
                wgt[index][(number, *here)] = value

        loop(times, step, times < 3)

    def pulled(level, field, x, blk, y, cy, centre):
        index = level.index
        here = (pl.ds(x, blk), pl.ds(y, cy), slice(None))
        weight = wgt[index]
        total = one[index][here] + weight[(0, *here)] * field[pl.ds(x + 1, blk), pl.ds(y, cy), :]
        other = weight[(1, *here)] * field[pl.ds(x - 1, blk), pl.ds(y, cy), :]
        total = total + weight[(2, *here)] * field[pl.ds(x, blk), pl.ds(y + 1, cy), :]
        other = other + weight[(3, *here)] * field[pl.ds(x, blk), pl.ds(y - 1, cy), :]
        total = total + weight[(4, *here)] * pltpu.roll(centre, 127, 2)
        other = other + weight[(5, *here)] * pltpu.roll(centre, 1, 2)
        return total + other

    def first_sweep(level):
        index = level.index
        first, blk, times = level.span(level.reach)

        def step(i):
            here = (pl.ds(first + i * blk, blk), pl.ds(*level.wide), slice(None))
            one[index][here] = inv[index][here] * right[index][here]

        loop(times, step, True)

    def sweep(level, source, target, radius):
        first, blk, times = level.span(radius)
        y, cy = level.mid if radius else level.core

        def step(i):
            x = first + i * blk
            here = (pl.ds(x, blk), pl.ds(y, cy), slice(None))
            centre = source[here]
            target[here] = 0.2 * centre + pulled(level, source, x, blk, y, cy, centre)

        loop(times, step, True)

    def residual(level, radius, columns):
        index = level.index
        first, blk, times = level.span(radius)
        y, cy = columns

        def step(i):
            x = first + i * blk
            here = (pl.ds(x, blk), pl.ds(y, cy), slice(None))
            centre = two[index][here]
            total = pulled(level, two[index], x, blk, y, cy, centre)
            tri[index][here] = dia[index][here] * (total - 0.8 * centre)

        loop(times, step, True)

    def lift(value, level, x, y, count):
        for row in (x, x + 1):
            for column in (y, y + 1):
                spot = (row, pl.ds(column, count, stride=2), slice(None))
                two[level.index][spot] = two[level.index][spot] + value

    zero, one_, two_, three, four, five = levels

    barrier = pltpu.get_barrier_semaphore()
    greeted = around(zero, zero.reach + 1) + ([(0, 2), (0, -2)] if gy_count > 4 else [])
    for dx, dy in greeted:
        pl.semaphore_signal(barrier, inc=1, device_id=device(dx, dy), device_id_type=MESH)
    pl.semaphore_wait(barrier, len(greeted))

    sent_tis = send_block(tis, zero, zero.reach + 1, (), 0, tis_ref)
    sent_src = send_block(right[0], zero, zero.reach, (), 0, src_ref)
    loads = []
    for position, (source, target) in enumerate(
        (
            (tis_ref, tis.at[zero.own_x, zero.own_y]),
            (src_ref, right[0].at[zero.own_x, zero.own_y]),
            (types_ref, table),
        )
    ):
        copy = pltpu.make_async_copy(source, target, local_sem.at[position])
        copy.start()
        loads.append(copy)
    for level in (three, four, five):
        index = level.index
        for ref in (coef[index].at[0], one[index], two[index], tri[index]):
            ref[:, pl.ds(0, 8), :] = jnp.zeros((level.nx, 8, 128), F32)
            ref[:, pl.ds(8 + level.columns, 8), :] = jnp.zeros((level.nx, 8, 128), F32)
    for copy in loads:
        copy.wait()
    loop(zero.rows // 2, lambda i: types(zero.ox + 2 * i, 2, zero.oy, zero.columns))

    def coarsen(fine, level, known):
        for field in (0, 1):

            def step(i):
                value = mean(
                    coef[fine.index],
                    (field,),
                    fine.ox + 2 * (i - known),
                    fine.oy - 2 * known,
                    level.columns + 2 * known,
                )
                here = (level.ox - known + i, pl.ds(level.oy - known, level.columns + 2 * known), slice(None))
                coef[level.index][(field, *here)] = value

            loop(level.rows + 2 * known, step)

    coarsen(zero, one_, 0)
    both = (slice(None),)
    sent_c1 = send_block(coef[1], one_, one_.reach + 1, both)
    weights(zero, (zero.ox + 1, (zero.rows - 2) // 2, 2), zero.core, True)

    arrived(sent_tis)
    ring = zero.reach + 1
    types(zero.ox - ring, ring, 8, zero.mid[1])
    types(zero.ox + zero.rows, ring, 8, zero.mid[1])
    types(zero.ox, zero.rows, 8, ring)
    types(zero.ox, zero.rows, zero.oy + zero.columns, ring)
    arrived(sent_src)
    weights(zero, (zero.ox - zero.reach, zero.reach + 1, 1), zero.wide, True)
    weights(zero, (zero.ox + zero.rows - 1, zero.reach + 1, 1), zero.wide, True)
    weights(zero, (zero.ox + 1, zero.rows - 2, 1), (8, 8), True)
    weights(zero, (zero.ox + 1, zero.rows - 2, 1), (zero.oy + zero.columns - 4, 8), True)

    def restrict_to(fine, level, known):
        def step(i):
            value = mean(tri[fine.index], (), fine.ox + 2 * (i - known), fine.oy - 2 * known, level.columns + 2 * known)
            right[level.index][level.ox - known + i, pl.ds(level.oy - known, level.columns + 2 * known), :] = value

        loop(level.rows + 2 * known, step, True)

    sweep(zero, one[0], two[0], zero.reach - 1)
    residual(zero, 0, zero.core)
    restrict_to(zero, one_, 0)
    sent_b1 = send_block(right[1], one_, one_.reach)
    left(sent_tis)
    left(sent_src)
    arrived(sent_c1)
    coarsen(one_, two_, 2)
    sent_c2 = send_block(coef[2], two_, two_.reach + 1, both, 2)
    weights(one_)
    left(sent_c1)

    arrived(sent_b1)
    first_sweep(one_)
    sweep(one_, one[1], two[1], one_.reach - 1)
    residual(one_, 2, one_.mid)
    restrict_to(one_, two_, 1)
    sent_b2 = send_block(right[2], two_, two_.reach, (), 1)
    arrived(sent_c2)
    for field in (0, 1):
        for row in range(4):
            gat_c[field, row] = mean(coef[2], (field,), two_.ox - 2 + 2 * row, two_.oy, 4)
    own_c3, sent_c3 = send_columns(gat_c, coef[3], three, ((0, -1),), 0, both)
    weights(two_)
    left(sent_c2)
    left(sent_b1)

    arrived(sent_b2)
    first_sweep(two_)
    sweep(two_, one[2], two[2], two_.reach - 1)
    residual(two_, 2, two_.core)
    for row in range(4):
        gat_b[row] = mean(tri[2], (), two_.ox - 2 + 2 * row, two_.oy, 4)

    own_b3, sent_b3 = send_columns(gat_b, right[3], three, ((2, -5), (-2, 3), (0, -1)), 1)
    own_c3.wait()
    arrived(sent_c3)
    sent_x3 = send_known(coef[3], three, ((2, -1, -5, 4), (-2, -1, 3, 4), (3, 0, -6, 1), (-3, 1, 7, 1)), 1, both)
    left(sent_b2)
    left(sent_c3)
    arrived(sent_x3)
    for row in range(-3, 4):
        for field in (0, 1):
            value = mean(coef[3], (field,), three.ox + 2 * row, 8, four.columns)
            coef[4][field, four.ox + row, four.own_y, :] = value
    sent_c4 = send_known(coef[4], four, ((3, -3, -6, 3), (-3, 1, 4, 3)), 1, both)
    weights(three)
    left(sent_x3)
    own_b3.wait()
    arrived(sent_b3)
    first_sweep(three)
    sweep(three, one[3], two[3], three.reach - 1)
    residual(three, 2, three.core)
    for row in (-1, 0, 1):
        right[4][four.ox + row, four.own_y, :] = mean(tri[3], (), three.ox + 2 * row, 8, four.columns)

    moves = ((4, -1, -5, 1), (-4, 1, 5, 1), (3, -1, -4, 3), (-3, -1, 2, 3))
    sent_r4 = send_known(right[4], four, moves)
    arrived(sent_c4)
    chip = four.ox - parity
    for row in range(-2, 3):
        for field in (0, 1):
            value = mean(coef[4], (field,), chip + 2 * row, 8, five.columns)
            coef[5][field, five.ox + row, five.own_y, :] = value
    sent_c5 = send_known(coef[5], five, ((4, -2, -6, 4), (-4, -1, 3, 4)), 2, both)
    weights(four)
    left(sent_b3)
    left(sent_c4)
    arrived(sent_r4)
    first_sweep(four)
    sweep(four, one[4], two[4], four.reach - 1)
    residual(four, 3, four.core)
    for row in (-1, 0, 1):
        right[5][five.ox + row, five.own_y, :] = mean(tri[4], (), chip + 2 * row, 8, five.columns)

    sent_r5 = send_known(right[5], five, moves, 2)
    arrived(sent_c5)
    weights(five)
    left(sent_r4)
    left(sent_c5)
    arrived(sent_r5)
    first_sweep(five)
    sweep(five, one[5], two[5], 4)
    sweep(five, two[5], tri[5], 3)
    sweep(five, tri[5], two[5], 2)
    left(sent_r5)

    def ascend(level, last):
        index = level.index
        sweep(level, two[index], tri[index], last + 1)
        sweep(level, tri[index], two[index], last)

    for offset in range(-4, 5):
        row = five.ox - 4 + (parity + (offset + 8)) // 2
        value = two[5][row, five.own_y, :]
        for column in (8, 9):
            spot = (four.ox + offset, pl.ds(column, five.columns, stride=2), slice(None))
            two[4][spot] = two[4][spot] + value
    ascend(four, 2)
    for offset in range(-2, 3):
        lift(two[4][four.ox + offset, four.own_y, :], three, three.ox + 2 * offset, 8, four.columns)
    ascend(three, 2)
    for offset in range(-2, 4):
        value = two[3][three.ox + offset, pl.ds(6 + 4 * gy, 8), :]
        lift(value, two_, two_.ox + 2 * offset, two_.oy - 4, 8)
    ascend(two_, 2)

    def lift_one(i):
        value = two[2][two_.ox - 2 + i, pl.ds(two_.oy - 2, two_.columns + 4), :]
        lift(value, one_, one_.ox - 4 + 2 * i, one_.oy - 4, two_.columns + 4)

    loop(two_.rows + 4, lift_one, True)
    ascend(one_, 1)

    def lift_zero(i):
        value = two[1][one_.ox - 1 + i, pl.ds(one_.oy - 1, one_.columns + 2), :]
        lift(value, zero, zero.ox - 2 + 2 * i, zero.oy - 2, one_.columns + 2)

    loop(one_.rows + 2, lift_zero, True)
    sweep(zero, two[0], tri[0], 1)
    y, cy = zero.core
    for row in range(0, zero.rows, 2):
        here = (pl.ds(zero.ox + row, 2), pl.ds(y, cy), slice(None))
        centre = tri[0][here]
        out_ref[pl.ds(row, 2)] = 0.2 * centre + pulled(zero, tri[0], zero.ox + row, 2, y, cy, centre)


def build(mesh, rows, columns):
    gx_count, gy_count = mesh.shape["gx"], mesh.shape["gy"]
    levels = [
        Level(0, rows, columns, False, 2),
        Level(1, rows // 2, columns // 2, False, 3),
        Level(2, rows // 4, columns // 4, False, 12),
        Level(3, rows // 8, columns // 8 * gy_count, True, 4),
        Level(4, rows // 16, columns // 16 * gy_count, True, 11),
        Level(5, 1, columns // 32 * gy_count, True, 11),
    ]
    zero = levels[0]
    messages = 96
    scratch = [pltpu.VMEM(zero.shape(), jnp.int32)]
    scratch += [pltpu.VMEM(level.shape(2), F32) for level in levels]
    scratch += [pltpu.VMEM(level.shape(), F32) for level in levels]
    scratch += [pltpu.VMEM(level.shape(6), F32) for level in levels]
    for _ in range(5):
        scratch += [pltpu.VMEM(level.shape(), F32) for level in levels]
    scratch += [
        pltpu.VMEM((2, 4, 4, 128), F32),
        pltpu.VMEM((4, 4, 128), F32),
        pltpu.SMEM((2 * TYPES,), F32),
        pltpu.SemaphoreType.DMA((4,)),
        pltpu.SemaphoreType.DMA((messages,)),
        pltpu.SemaphoreType.DMA((messages,)),
    ]
    return pl.pallas_call(
        functools.partial(kernel, (gx_count, gy_count), levels),
        out_shape=jax.ShapeDtypeStruct((rows, columns, 128), F32),
        in_specs=[
            pl.BlockSpec(memory_space=pltpu.HBM),
            pl.BlockSpec(memory_space=pltpu.HBM),
            pl.BlockSpec(memory_space=pltpu.HBM),
        ],
        out_specs=pl.BlockSpec(memory_space=pltpu.VMEM),
        scratch_shapes=scratch,
        name="vcycle",
        compiler_params=pltpu.CompilerParams(
            collective_id=0, has_side_effects=True, vmem_limit_bytes=56_250_000
        ),
    )


def solution(mesh):
    def body(source, tissue, diffusivity, uptake):
        call = build(mesh, source.shape[0], source.shape[1])
        return call(source, tissue, jnp.concatenate([diffusivity, uptake]))

    in_specs = (P("gx", "gy", None), P("gx", "gy", None), P(), P())
    out_specs = P("gx", "gy", None)
    return jax.shard_map(body, mesh=mesh, in_specs=in_specs, out_specs=out_specs, check_vma=False)
```

```python
import functools

import jax
import jax.numpy as jnp
from jax import lax
from jax.experimental import pallas as pl
from jax.experimental.pallas import tpu as pltpu
from jax.sharding import PartitionSpec as P

MESH = pl.DeviceIdType.MESH
F32 = jnp.float32
LEVELS = 6
TYPES = 8
HZ = 0.5 * 0.015625
REACH = (3, 4, 5, 5, 5, 5)


class Level:
    def __init__(self, index, rows, columns, across, most):
        self.index, self.rows, self.columns, self.across, self.most = index, rows, columns, across, most
        self.reach = REACH[index]
        self.ox = self.reach + 1
        self.nx = rows + 2 * self.ox + 2
        if across:
            self.oy = 8
            self.wide = self.mid = self.core = (8, columns)
            self.ny = 8 + columns + 8
        else:
            self.oy = 12
            self.core = (12, columns)
            around = -(-(columns + 8) // 8) * 8
            self.mid = (8, around)
            self.wide = (8, around) if self.reach < 5 else (4, around + 8)
            self.ny = around + 16
        self.own_x = pl.ds(self.ox, rows)
        self.own_y = pl.ds(self.oy, columns)
        self.half = 0.5 * 0.25**index

    def shape(self, *lead):
        return (*lead, self.nx, self.ny, 128)

    def span(self, radius):
        count = self.rows + 2 * radius
        times = -(-count // self.most)
        return self.ox - radius, -(-count // times), times


def overlap(size, step, radius, known):
    if known:
        low, high = {1: (-radius, -known), 0: (-known, size + known), -1: (size + known, size + radius)}[step]
        return low + step * size, low, high - low
    low = max(-radius, -step * size)
    high = min(size + radius, (1 - step) * size)
    return low + step * size, low, high - low


def kernel(sizes, levels, src_ref, tis_ref, types_ref, out_ref, *scratch):
    gx_count, gy_count = sizes
    names = iter(scratch)
    tis = next(names)
    coef = [next(names) for _ in levels]
    right = [next(names) for _ in levels]
    wgt = [next(names) for _ in levels]
    inv = [next(names) for _ in levels]
    dia = [next(names) for _ in levels]
    one = [next(names) for _ in levels]
    two = [next(names) for _ in levels]
    tri = [next(names) for _ in levels]
    gat_c, gat_b = next(names), next(names)
    table = next(names)
    local_sem, send_sem, recv_sem = next(names), next(names), next(names)

    gx = lax.axis_index("gx")
    gy = lax.axis_index("gy")
    parity = lax.rem(gx, 2)
    places = {}

    def device(dx, dy):
        if ("x", dx) not in places:
            places["x", dx] = lax.rem(gx + (dx + gx_count), gx_count) if dx else gx
        if ("y", dy) not in places:
            places["y", dy] = lax.rem(gy + (dy + gy_count), gy_count) if dy else gy
        return places["x", dx], places["y", dy]

    counter = [0]

    def remote(source, target, dx, dy):
        number = counter[0]
        counter[0] += 1
        copy = pltpu.make_async_remote_copy(
            src_ref=source,
            dst_ref=target,
            send_sem=send_sem.at[number],
            recv_sem=recv_sem.at[number],
            device_id=device(dx, dy),
            device_id_type=MESH,
        )
        copy.start()
        return copy

    def arrived(copies):
        for copy in copies:
            copy.wait_recv()

    def left(copies):
        for copy in copies:
            copy.wait_send()

    def around(level, radius, known=0):
        far = -(-(radius - known) // level.rows)
        return [(dx, dy) for dx in range(-far, far + 1) for dy in (-1, 0, 1) if (dx, dy) != (0, 0)]

    def send_block(ref, level, radius, lead=(), known=0, origin=None):
        copies = []
        for dx, dy in sorted(around(level, radius, known), key=lambda step: -abs(step[0]) - abs(step[1])):
            sx, tx, cx = overlap(level.rows, dx, radius, known)
            sy, ty, cy = overlap(level.columns, dy, radius, known)
            if origin is None:
                source = ref.at[(*lead, pl.ds(level.ox + sx, cx), pl.ds(level.oy + sy, cy))]
            else:
                source = origin.at[pl.ds(sx, cx), pl.ds(sy, cy)]
            target = ref.at[(*lead, pl.ds(level.ox + tx, cx), pl.ds(level.oy + ty, cy))]
            copies.append(remote(source, target, dx, dy))
        return copies

    def send_known(ref, level, moves, stride=1, lead=()):
        copies = []
        for step, sx, tx, cx in moves:
            source = ref.at[(*lead, pl.ds(level.ox + sx, cx), level.own_y)]
            target = ref.at[(*lead, pl.ds(level.ox + tx, cx), level.own_y)]
            copies.append(remote(source, target, step * stride, 0))
        return copies

    def send_columns(source, ref, level, moves, position, lead=()):
        columns = pl.ds(8 + 4 * gy, 4)
        target = ref.at[(*lead, pl.ds(level.ox - 1, 4), columns)]
        own = pltpu.make_async_copy(source, target, local_sem.at[position])
        own.start()
        copies = []
        for dy in sorted(range(gy_count), key=lambda step: -min(step, gy_count - step)):
            for dx, tx in moves:
                if dx or dy:
                    target = ref.at[(*lead, pl.ds(level.ox + tx, 4), columns)]
                    copies.append(remote(source, target, dx, dy))
        return own, copies

    def loop(count, step, unrolled=False):
        if unrolled:
            for i in range(count):
                step(i)
            return

        def body(i, carry):
            step(i)
            return carry

        lax.fori_loop(0, count, body, 0)

    def seam(level, shape, axis, start, last):
        if axis == 0:
            half = level.index == LEVELS - 1
            total = level.rows * (gx_count // 2 if half else gx_count)
            base = (gx // 2 if half else gx) * level.rows + start - level.ox
        else:
            total = level.columns * gy_count
            base = gy * level.columns + start - level.oy
        place = lax.broadcasted_iota(jnp.int32, shape, axis) + base
        if last:
            return (place == total - 1) | (place == -1)
        return (place == 0) | (place == total)

    def types(x, blk, y, cy):
        kind = tis[pl.ds(x, blk), pl.ds(y, cy), :]
        kappa = jnp.full(kind.shape, table[0], F32)
        sigma = jnp.full(kind.shape, table[TYPES], F32)
        for index in range(1, TYPES):
            hit = kind == index
            kappa = jnp.where(hit, table[index], kappa)
            sigma = jnp.where(hit, table[TYPES + index], sigma)
        coef[0][0, pl.ds(x, blk), pl.ds(y, cy), :] = kappa
        coef[0][1, pl.ds(x, blk), pl.ds(y, cy), :] = sigma

    def mean(ref, lead, x, y, count):
        even = pl.ds(y, count, stride=2)
        odd = pl.ds(y + 1, count, stride=2)
        near = ref[(*lead, x, even, slice(None))] + ref[(*lead, x + 1, even, slice(None))]
        far = ref[(*lead, x, odd, slice(None))] + ref[(*lead, x + 1, odd, slice(None))]
        return 0.25 * (near + far)

    def weights(level, rows=None, columns=None, start=False):
        index = level.index
        first, blk, times = rows or level.span(level.reach)
        y, cy = columns or level.wide
        half = level.half

        def step(i):
            x = first + i * blk
            here = (pl.ds(x, blk), pl.ds(y, cy), slice(None))
            field = coef[index].at[0]
            centre = field[here]
            plane = lax.broadcasted_iota(jnp.int32, centre.shape, 2)
            row, column = pl.ds(x, blk), pl.ds(y, cy)
            faces = [
                (half, field[pl.ds(x + 1, blk), column, :], seam(level, centre.shape, 0, x, True)),
                (half, field[pl.ds(x - 1, blk), column, :], seam(level, centre.shape, 0, x, False)),
            ]
            if level.across:
                faces += [
                    (half, field[row, pl.ds(y + 1, cy), :], None),
                    (half, field[row, pl.ds(y - 1, cy), :], None),
                ]
            else:
                faces += [
                    (half, field[row, pl.ds(y + 1, cy), :], seam(level, centre.shape, 1, y, True)),
                    (half, field[row, pl.ds(y - 1, cy), :], seam(level, centre.shape, 1, y, False)),
                ]
            faces += [
                (HZ, pltpu.roll(centre, 127, 2), plane == 127),
                (HZ, pltpu.roll(centre, 1, 2), plane == 0),
            ]
            diag = coef[index][(1, *here)]
            weight = []
            for scale, beyond, closed in faces:
                if closed is not None:
                    beyond = jnp.where(closed, 0.0, beyond)
                face = scale * (centre + beyond)
                diag = diag + face
                weight.append(face)
            inverse = 0.8 / diag
            dia[index][here] = 1.25 * diag
            if start:
                one[index][here] = inverse * right[index][here]
            else:
                inv[index][here] = inverse
            for number, (scale, beyond, closed) in enumerate(faces):
                value = inverse * weight[number]
                if closed is not None:
                    value = jnp.where(closed, 0.0, value)
                wgt[index][(number, *here)] = value

        loop(times, step, times < 3)

    def pulled(level, field, x, blk, y, cy, centre):
        index = level.index
        here = (pl.ds(x, blk), pl.ds(y, cy), slice(None))
        weight = wgt[index]
        total = one[index][here] + weight[(0, *here)] * field[pl.ds(x + 1, blk), pl.ds(y, cy), :]
        other = weight[(1, *here)] * field[pl.ds(x - 1, blk), pl.ds(y, cy), :]
        total = total + weight[(2, *here)] * field[pl.ds(x, blk), pl.ds(y + 1, cy), :]
        other = other + weight[(3, *here)] * field[pl.ds(x, blk), pl.ds(y - 1, cy), :]
        total = total + weight[(4, *here)] * pltpu.roll(centre, 127, 2)
        other = other + weight[(5, *here)] * pltpu.roll(centre, 1, 2)
        return total + other

    def first_sweep(level):
        index = level.index
        first, blk, times = level.span(level.reach)

        def step(i):
            here = (pl.ds(first + i * blk, blk), pl.ds(*level.wide), slice(None))
            one[index][here] = inv[index][here] * right[index][here]

        loop(times, step, True)

    def sweep(level, source, target, radius):
        first, blk, times = level.span(radius)
        y, cy = level.mid if radius else level.core

        def step(i):
            x = first + i * blk
            here = (pl.ds(x, blk), pl.ds(y, cy), slice(None))
            centre = source[here]
            target[here] = 0.2 * centre + pulled(level, source, x, blk, y, cy, centre)

        loop(times, step, True)

    def residual(level, radius, columns):
        index = level.index
        first, blk, times = level.span(radius)
        y, cy = columns

        def step(i):
            x = first + i * blk
            here = (pl.ds(x, blk), pl.ds(y, cy), slice(None))
            centre = two[index][here]
            total = pulled(level, two[index], x, blk, y, cy, centre)
            tri[index][here] = dia[index][here] * (total - 0.8 * centre)

        loop(times, step, True)

    def lift(value, level, x, y, count):
        for row in (x, x + 1):
            for column in (y, y + 1):
                spot = (row, pl.ds(column, count, stride=2), slice(None))
                two[level.index][spot] = two[level.index][spot] + value

    zero, one_, two_, three, four, five = levels

    barrier = pltpu.get_barrier_semaphore()
    greeted = around(zero, zero.reach + 1) + ([(0, 2), (0, -2)] if gy_count > 4 else [])
    for dx, dy in greeted:
        pl.semaphore_signal(barrier, inc=1, device_id=device(dx, dy), device_id_type=MESH)
    pl.semaphore_wait(barrier, len(greeted))

    sent_tis = send_block(tis, zero, zero.reach + 1, (), 0, tis_ref)
    sent_src = send_block(right[0], zero, zero.reach, (), 0, src_ref)
    loads = []
    for position, (source, target) in enumerate(
        (
            (tis_ref, tis.at[zero.own_x, zero.own_y]),
            (src_ref, right[0].at[zero.own_x, zero.own_y]),
            (types_ref, table),
        )
    ):
        copy = pltpu.make_async_copy(source, target, local_sem.at[position])
        copy.start()
        loads.append(copy)
    for level in (three, four, five):
        index = level.index
        for ref in (coef[index].at[0], one[index], two[index], tri[index]):
            ref[:, pl.ds(0, 8), :] = jnp.zeros((level.nx, 8, 128), F32)
            ref[:, pl.ds(8 + level.columns, 8), :] = jnp.zeros((level.nx, 8, 128), F32)
    for copy in loads:
        copy.wait()
    loop(zero.rows // 2, lambda i: types(zero.ox + 2 * i, 2, zero.oy, zero.columns))

    def coarsen(fine, level, known):
        for field in (0, 1):

            def step(i):
                value = mean(
                    coef[fine.index],
                    (field,),
                    fine.ox + 2 * (i - known),
                    fine.oy - 2 * known,
                    level.columns + 2 * known,
                )
                here = (level.ox - known + i, pl.ds(level.oy - known, level.columns + 2 * known), slice(None))
                coef[level.index][(field, *here)] = value

            loop(level.rows + 2 * known, step)

    coarsen(zero, one_, 0)
    both = (slice(None),)
    sent_c1 = send_block(coef[1], one_, one_.reach + 1, both)
    weights(zero, (zero.ox + 1, (zero.rows - 2) // 2, 2), zero.core, True)

    arrived(sent_tis)
    ring = zero.reach + 1
    types(zero.ox - ring, ring, 8, zero.mid[1])
    types(zero.ox + zero.rows, ring, 8, zero.mid[1])
    types(zero.ox, zero.rows, 8, ring)
    types(zero.ox, zero.rows, zero.oy + zero.columns, ring)
    arrived(sent_src)
    weights(zero, (zero.ox - zero.reach, zero.reach + 1, 1), zero.wide, True)
    weights(zero, (zero.ox + zero.rows - 1, zero.reach + 1, 1), zero.wide, True)
    weights(zero, (zero.ox + 1, zero.rows - 2, 1), (8, 8), True)
    weights(zero, (zero.ox + 1, zero.rows - 2, 1), (zero.oy + zero.columns - 4, 8), True)

    def restrict_to(fine, level, known):
        def step(i):
            value = mean(tri[fine.index], (), fine.ox + 2 * (i - known), fine.oy - 2 * known, level.columns + 2 * known)
            right[level.index][level.ox - known + i, pl.ds(level.oy - known, level.columns + 2 * known), :] = value

        loop(level.rows + 2 * known, step, True)

    sweep(zero, one[0], two[0], zero.reach - 1)
    residual(zero, 0, zero.core)
    restrict_to(zero, one_, 0)
    sent_b1 = send_block(right[1], one_, one_.reach)
    left(sent_tis)
    left(sent_src)
    arrived(sent_c1)
    coarsen(one_, two_, 2)
    sent_c2 = send_block(coef[2], two_, two_.reach + 1, both, 2)
    weights(one_)
    left(sent_c1)

    arrived(sent_b1)
    first_sweep(one_)
    sweep(one_, one[1], two[1], one_.reach - 1)
    residual(one_, 2, one_.mid)
    restrict_to(one_, two_, 1)
    sent_b2 = send_block(right[2], two_, two_.reach, (), 1)
    arrived(sent_c2)
    for field in (0, 1):
        for row in range(4):
            gat_c[field, row] = mean(coef[2], (field,), two_.ox - 2 + 2 * row, two_.oy, 4)
    own_c3, sent_c3 = send_columns(gat_c, coef[3], three, ((0, -1),), 0, both)
    weights(two_)
    left(sent_c2)
    left(sent_b1)

    arrived(sent_b2)
    own_c3.wait()
    arrived(sent_c3)
    sent_x3 = send_known(coef[3], three, ((2, -1, -5, 4), (-2, -1, 3, 4)), 1, both)
    sent_x3 = sent_x3 + send_known(coef[3], three, ((3, 0, -6, 1), (-3, 1, 7, 1)), 1, both)
    first_sweep(two_)
    sweep(two_, one[2], two[2], two_.reach - 1)
    residual(two_, 2, two_.core)
    for row in range(4):
        gat_b[row] = mean(tri[2], (), two_.ox - 2 + 2 * row, two_.oy, 4)

    own_b3, sent_b3 = send_columns(gat_b, right[3], three, ((2, -5), (-2, 3), (0, -1)), 1)
    left(sent_b2)
    left(sent_c3)
    arrived(sent_x3)
    for row in range(-3, 4):
        for field in (0, 1):
            value = mean(coef[3], (field,), three.ox + 2 * row, 8, four.columns)
            coef[4][field, four.ox + row, four.own_y, :] = value
    sent_c4 = send_known(coef[4], four, ((3, -3, -6, 3), (-3, 1, 4, 3)), 1, both)
    weights(three)
    left(sent_x3)
    own_b3.wait()
    arrived(sent_b3)
    first_sweep(three)
    sweep(three, one[3], two[3], three.reach - 1)
    residual(three, 2, three.core)
    for row in (-1, 0, 1):
        right[4][four.ox + row, four.own_y, :] = mean(tri[3], (), three.ox + 2 * row, 8, four.columns)

    moves = ((4, -1, -5, 1), (-4, 1, 5, 1), (3, -1, -4, 3), (-3, -1, 2, 3))
    sent_r4 = send_known(right[4], four, moves)
    arrived(sent_c4)
    chip = four.ox - parity
    for row in range(-2, 3):
        for field in (0, 1):
            value = mean(coef[4], (field,), chip + 2 * row, 8, five.columns)
            coef[5][field, five.ox + row, five.own_y, :] = value
    sent_c5 = send_known(coef[5], five, ((4, -2, -6, 4), (-4, -1, 3, 4)), 2, both)
    weights(four)
    left(sent_b3)
    left(sent_c4)
    arrived(sent_r4)
    first_sweep(four)
    sweep(four, one[4], two[4], four.reach - 1)
    residual(four, 3, four.core)
    for row in (-1, 0, 1):
        right[5][five.ox + row, five.own_y, :] = mean(tri[4], (), chip + 2 * row, 8, five.columns)

    sent_r5 = send_known(right[5], five, moves, 2)
    arrived(sent_c5)
    weights(five)
    left(sent_r4)
    left(sent_c5)
    arrived(sent_r5)
    first_sweep(five)
    sweep(five, one[5], two[5], 4)
    sweep(five, two[5], tri[5], 3)
    sweep(five, tri[5], two[5], 2)
    left(sent_r5)

    def ascend(level, last):
        index = level.index
        sweep(level, two[index], tri[index], last + 1)
        sweep(level, tri[index], two[index], last)

    for offset in range(-4, 5):
        row = five.ox - 4 + (parity + (offset + 8)) // 2
        value = two[5][row, five.own_y, :]
        for column in (8, 9):
            spot = (four.ox + offset, pl.ds(column, five.columns, stride=2), slice(None))
            two[4][spot] = two[4][spot] + value
    ascend(four, 2)
    for offset in range(-2, 3):
        lift(two[4][four.ox + offset, four.own_y, :], three, three.ox + 2 * offset, 8, four.columns)
    ascend(three, 2)
    for offset in range(-2, 4):
        value = two[3][three.ox + offset, pl.ds(6 + 4 * gy, 8), :]
        lift(value, two_, two_.ox + 2 * offset, two_.oy - 4, 8)
    ascend(two_, 2)

    def lift_one(i):
        value = two[2][two_.ox - 2 + i, pl.ds(two_.oy - 2, two_.columns + 4), :]
        lift(value, one_, one_.ox - 4 + 2 * i, one_.oy - 4, two_.columns + 4)

    loop(two_.rows + 4, lift_one, True)
    ascend(one_, 1)

    def lift_zero(i):
        value = two[1][one_.ox - 1 + i, pl.ds(one_.oy - 1, one_.columns + 2), :]
        lift(value, zero, zero.ox - 2 + 2 * i, zero.oy - 2, one_.columns + 2)

    loop(one_.rows + 2, lift_zero, True)
    sweep(zero, two[0], tri[0], 1)
    y, cy = zero.core
    for row in range(0, zero.rows, 2):
        here = (pl.ds(zero.ox + row, 2), pl.ds(y, cy), slice(None))
        centre = tri[0][here]
        out_ref[pl.ds(row, 2)] = 0.2 * centre + pulled(zero, tri[0], zero.ox + row, 2, y, cy, centre)


def build(mesh, rows, columns):
    gx_count, gy_count = mesh.shape["gx"], mesh.shape["gy"]
    levels = [
        Level(0, rows, columns, False, 2),
        Level(1, rows // 2, columns // 2, False, 3),
        Level(2, rows // 4, columns // 4, False, 12),
        Level(3, rows // 8, columns // 8 * gy_count, True, 4),
        Level(4, rows // 16, columns // 16 * gy_count, True, 11),
        Level(5, 1, columns // 32 * gy_count, True, 11),
    ]
    zero = levels[0]
    messages = 96
    scratch = [pltpu.VMEM(zero.shape(), jnp.int32)]
    scratch += [pltpu.VMEM(level.shape(2), F32) for level in levels]
    scratch += [pltpu.VMEM(level.shape(), F32) for level in levels]
    scratch += [pltpu.VMEM(level.shape(6), F32) for level in levels]
    for _ in range(5):
        scratch += [pltpu.VMEM(level.shape(), F32) for level in levels]
    scratch += [
        pltpu.VMEM((2, 4, 4, 128), F32),
        pltpu.VMEM((4, 4, 128), F32),
        pltpu.SMEM((2 * TYPES,), F32),
        pltpu.SemaphoreType.DMA((4,)),
        pltpu.SemaphoreType.DMA((messages,)),
        pltpu.SemaphoreType.DMA((messages,)),
    ]
    return pl.pallas_call(
        functools.partial(kernel, (gx_count, gy_count), levels),
        out_shape=jax.ShapeDtypeStruct((rows, columns, 128), F32),
        in_specs=[
            pl.BlockSpec(memory_space=pltpu.HBM),
            pl.BlockSpec(memory_space=pltpu.HBM),
            pl.BlockSpec(memory_space=pltpu.HBM),
        ],
        out_specs=pl.BlockSpec(memory_space=pltpu.VMEM),
        scratch_shapes=scratch,
        name="vcycle",
        compiler_params=pltpu.CompilerParams(
            collective_id=0, has_side_effects=True, vmem_limit_bytes=56_250_000
        ),
    )


def solution(mesh):
    def body(source, tissue, diffusivity, uptake):
        call = build(mesh, source.shape[0], source.shape[1])
        return call(source, tissue, jnp.concatenate([diffusivity, uptake]))

    in_specs = (P("gx", "gy", None), P("gx", "gy", None), P(), P())
    out_specs = P("gx", "gy", None)
    return jax.shard_map(body, mesh=mesh, in_specs=in_specs, out_specs=out_specs, check_vma=False)
```
